128 devices in a mesh: dp: 32 (over x, z, core), tp: 4 (over y).
Axes of the slice: x: 4, y: 4, z: 4, core: 2. Of those that a mesh axis runs over, the one named last changes fastest.
Arguments:
- node_embed: bfloat16 [3, 32, 8, 7168], P(None, 'dp', None, 'tp'), may hold values from -8 to 8
- embed_gain: float32 [7168], P('tp'), may hold values from 0.3 to 4.5
- root_hidden: bfloat16 [32, 7168], P('dp', 'tp'), may hold values from -6 to 6
- parents: int32 [2, 32, 8], P(None, 'dp'), may hold values from 0 to 7
- queries: bfloat16 [3, 32, 8, 128, 576], P(None, 'dp', None, 'tp'), may hold values from -24 to 24
- cache: bfloat16 [32, 4096, 576], P('dp'), may hold values from -4 to 4
- cache_len: int32 [32], P('dp'), may hold values from 512 to 4096, as said below
- value_up: bfloat16 [128, 512, 128], P('tp'), may hold values from -1 to 1
- out_proj: bfloat16 [16384, 7168], P('tp', 'dp'), may hold values from -0.046875 to 0.046875
- moe_gain: float32 [7168], P('tp'), may hold values from 0.1 to 1.9
- router: bfloat16 [7168, 32], P('tp'), may hold values from -0.0625 to 0.0625
- expert_ids: int32 [3, 32, 8, 8], P(None, 'dp'), may hold values from 0 to 31, all different within a row; in each aligned block of 8 rows (0 to 7, 8 to 15, ..., all dimensions but the last counted through in order) at most 4 rows name the same one
- w_gate: bfloat16 [32, 7168, 1024], P('dp', None, 'tp'), may hold values from -0.0625 to 0.0625
- w_up: bfloat16 [32, 7168, 1024], P('dp', None, 'tp'), may hold values from -0.0625 to 0.0625
- w_down: bfloat16 [32, 1024, 7168], P('dp', 'tp'), may hold values from -0.1875 to 0.1875
Outputs:
- drafted: bfloat16 [3, 32, 8, 7168], P(None, 'dp', None, 'tp')
The draws below stay inside these ranges and needn't reach their ends.
Inputs may be any that keep to these rules, and one draw needn't show every extreme that they name: `cache_len`: request 0 holds exactly 4096 cached tokens. `expert_ids`: each node names 8 different experts. At one depth the nodes of the 1 request of one index of dp name no expert more than 4 times, and in some of these blocks an expert is named exactly 4 times.
All inputs are finite; a program needn't handle non-finite values.
Results may differ from the reference program's by a relative error of at most 0.017.
Values may be sent and summed in bfloat16 or wider, within the bound.
No kernel may reach another device: no remote copies, remote signals or barrier semaphores. Data moves between devices by JAX's collectives and lax.ppermute only.
A program may use at most 128 MiB of HBM per device.

```python
import math
import jax
import jax.numpy as jnp
import numpy as np
from jax import lax

D = 7168
HEADS = 128
LATENT = 512
ROPE = 64
HEAD_DIM = 128
TOP = 8
FFE = 1024
NODES = 8
DEPTHS = 3
CACHE = 4096
REQ_DEV = 1
REQUESTS = 32
EXPERTS = 32
CAP = 4
QK = 576
N_DP = 32


def draw_cache(key, part):
    key = jax.random.fold_in(key, 11)
    base_key = jax.random.fold_in(key, 1)
    base = jnp.clip(jax.random.normal(base_key, (REQUESTS, CACHE, QK), jnp.float32), -4.0, 4.0)
    return base.astype(jnp.bfloat16)


def draw_queries(key, part):
    key = jax.random.fold_in(key, 12)
    shape = (DEPTHS, REQUESTS, NODES, HEADS, QK)
    fresh = jnp.clip(jax.random.normal(key, shape, jnp.float32), -4.0, 4.0)
    return fresh.astype(jnp.bfloat16)


def draw_node_embed(key, part):
    key = jax.random.fold_in(key, 13)
    row_key, column_key, base_key = jax.random.split(key, 3)
    shape = (DEPTHS, REQUESTS, NODES, D)
    row_scale = jnp.exp(jax.random.uniform(row_key, (DEPTHS, REQUESTS, NODES, 1), jnp.float32, -1.15, 1.15))
    column_scale = jnp.exp(jax.random.uniform(column_key, (D,), jnp.float32, -1.15, 1.15))
    position = jnp.arange(D).astype(jnp.float32) / D
    base = jax.random.normal(base_key, shape, jnp.float32)
    column_scale = column_scale * 3.0 ** position
    return jnp.clip(base * row_scale * column_scale, -8.0, 8.0).astype(jnp.bfloat16)


def draw_embed_gain(key, part):
    key = jax.random.fold_in(key, 14)
    rough = jax.random.uniform(key, (D,), jnp.float32, 0.8, 1.25)
    position = jnp.arange(D).astype(jnp.float32) / D
    return 0.6 * 3.0 ** position * rough


def draw_cache_len(key, part):
    key = jax.random.fold_in(key, 15)
    lengths = jax.random.randint(key, (REQUESTS,), CACHE // 8, CACHE + 1, jnp.int32)
    return jnp.where(jnp.arange(REQUESTS) == 0, CACHE, lengths).astype(jnp.int32)


def set_ends(result, stream_key, least, high):
    longest = result.shape.index(max(result.shape))
    spots = []
    for shift in (0, 1):
        where = [jax.random.randint(jax.random.fold_in(stream_key, axis), (), 0, length) for axis, length in enumerate(result.shape)]
        where[longest] = (where[longest] + shift) % result.shape[longest]
        spots.append(tuple(where))
    return result.at[spots[0]].set(least).at[spots[1]].set(high)


def block_scale(rng, dims, cuts, smallest, largest):
    def one(dim, shards_of):
        heights = jax.random.uniform(jax.random.fold_in(jax.random.fold_in(rng, 6), dim), (shards_of,), jnp.float32, smallest / len(cuts), largest / len(cuts))
        return jnp.repeat(jnp.exp(heights), dims[dim] // shards_of).reshape((-1,) + (1,) * (len(dims) - dim - 1))

    factor_of = one(*cuts[0])
    for cut in cuts[1:]:
        factor_of = factor_of * one(*cut)
    return factor_of


def routed_block(rng, own, number, rows, amount, top, reach, lean):
    sequence = jax.random.permutation(rng, amount)
    packed, common = shares(amount, rows * top, reach, lean, True), shares(amount, rows * top, reach, lean, False)
    places = jnp.arange(amount)

    def named(sizes, rotation):
        used = int((sizes > 0).sum())
        fixed = max(1, used // 4)
        moved = fixed + (places - fixed + rotation * (used - fixed)) % max(1, amount - fixed)
        return jnp.zeros((amount,), jnp.int32).at[sequence[jnp.where(places < fixed, places, moved)]].set(jnp.asarray(sizes, jnp.int32))

    sizes = jnp.where(number % 4 == 0, named(packed, number // 4), named(common, number - number // 4 - 1))
    mixed = jax.random.permutation(jax.random.fold_in(own, 3), amount)
    giver, taker = mixed[0:amount // 2 * 2:2], mixed[1:amount // 2 * 2:2]
    margin = jnp.minimum(sizes[giver] - 1, reach - sizes[taker]) // 2
    margin = jnp.where((giver == sequence[0]) | (taker == sequence[0]) | (sizes[taker] == 0), 0, jnp.maximum(margin, 0))
    moved = jax.random.randint(jax.random.fold_in(own, 4), (amount // 2,), 0, 1 << 20) % (margin + 1)
    sizes = sizes.at[giver].add(-moved).at[taker].add(moved)
    labels = jnp.searchsorted(jnp.cumsum(sizes), jnp.arange(rows * top), side="right").astype(jnp.int32)
    listing = labels.reshape(top, rows).T
    listing = listing[jax.random.permutation(jax.random.fold_in(own, 1), rows)]
    rotation = jax.random.randint(jax.random.fold_in(own, 2), (rows, 1), 0, top)
    return jnp.take_along_axis(listing, (jnp.arange(top)[None, :] + rotation) % top, axis=1)


def shares(amount, total, most, lean, full):
    loads = [(1 << 20) // math.isqrt(grade ** lean) + 1 for grade in range(1, amount + 1)]
    largest = most if full else min(most, max(-(-total // amount), total * loads[0] // sum(loads)))
    least = 1 if total - largest >= amount - 1 else 0
    holding, surplus = [largest] + [least] * (amount - 1), total - largest - least * (amount - 1)
    while surplus > 0:
        free = [i for i in range(1, amount) if holding[i] < largest] or [i for i in range(1, amount) if holding[i] < most]
        whole, budget = sum([loads[i] for i in free]), surplus
        for i in free:
            more = min(most - holding[i], max(1, budget * loads[i] // whole), surplus)
            holding[i] = holding[i] + more
            surplus = surplus - more
    return np.array(holding)


def normal_values(key, dims, scale, limit, shards=(), held_as=jnp.bfloat16):
    factor_of = block_scale(key, dims, shards, -0.22, 0.18) if shards else 1.0
    drawn = jax.random.normal(key, dims, jnp.float32) * scale * factor_of
    return jnp.minimum(jnp.maximum(drawn, -limit), limit).astype(held_as)


def setup_inputs(seed: int = 0) -> dict:
    arg_keys = jax.random.split(jax.random.key(seed), 16)
    node_embed = draw_node_embed(jax.random.fold_in(arg_keys[15], 71), 0)
    embed_gain = draw_embed_gain(jax.random.fold_in(arg_keys[15], 71), 0)
    root_hidden = normal_values(arg_keys[2], (REQUESTS, D), 1.0, 6.0, ((0, 32), (1, 4)))
    parents = set_ends(jax.random.randint(arg_keys[3], (DEPTHS - 1, REQUESTS, NODES), 0, NODES), jax.random.fold_in(arg_keys[3], 1), 0, NODES - 1).astype(jnp.int32)
    queries = draw_queries(jax.random.fold_in(arg_keys[15], 71), 0)
    cache = draw_cache(jax.random.fold_in(arg_keys[15], 71), 0)
    cache_len = draw_cache_len(jax.random.fold_in(arg_keys[15], 71), 0)
    value_up = normal_values(arg_keys[7], (HEADS, LATENT, HEAD_DIM), (LATENT // 16) ** -0.5, 1.0, ((0, 4),))
    out_proj = normal_values(arg_keys[8], (HEADS * HEAD_DIM, D), (HEADS * HEAD_DIM) ** -0.5, 0.046875, ((0, 4), (1, 32)))
    moe_gain = jnp.clip(1.0 + 0.18 * jax.random.normal(arg_keys[9], (D,), jnp.float32), 0.1, 1.9)
    router = normal_values(arg_keys[10], (D, EXPERTS), D ** -0.5, 0.0625, ((0, 4),))
    expert_ids_keys = jax.random.split(jax.random.fold_in(arg_keys[11], 1), DEPTHS * REQUESTS * NODES // (REQ_DEV * NODES))
    expert_ids_turns = jax.random.permutation(jax.random.fold_in(arg_keys[11], 3), DEPTHS * REQUESTS * NODES // (REQ_DEV * NODES))
    expert_ids = jax.vmap(lambda own, number: routed_block(jax.random.fold_in(arg_keys[11], 2), own, number, REQ_DEV * NODES, EXPERTS, TOP, CAP, 2))(expert_ids_keys, expert_ids_turns).reshape((DEPTHS, REQUESTS, NODES, TOP))
    w_gate = normal_values(arg_keys[12], (EXPERTS, D, FFE), D ** -0.5, 0.0625, ((0, 32), (2, 4)))
    w_up = normal_values(arg_keys[13], (EXPERTS, D, FFE), D ** -0.5, 0.0625, ((0, 32), (2, 4)))
    w_down = normal_values(arg_keys[14], (EXPERTS, FFE, D), FFE ** -0.5, 0.1875, ((0, 32), (1, 4)))
    return {"node_embed": node_embed, "embed_gain": embed_gain, "root_hidden": root_hidden, "parents": parents, "queries": queries, "cache": cache, "cache_len": cache_len, "value_up": value_up, "out_proj": out_proj, "moe_gain": moe_gain, "router": router, "expert_ids": expert_ids, "w_gate": w_gate, "w_up": w_up, "w_down": w_down}


EPS = 1e-06
ROUTE_SCALE = 2.5

def attend_request(query_block, cache_block, length, value_up):
    query_rows = query_block.reshape(-1, LATENT + ROPE)
    scores = jnp.dot(query_rows, cache_block.T, preferred_element_type=jnp.float32) * (HEAD_DIM + ROPE) ** (-0.5)
    valid = jnp.arange(CACHE, dtype=jnp.int32) < length
    scores = jnp.where(valid[None, :], scores, -jnp.inf)
    highest = lax.optimization_barrier(jnp.max(scores, axis=1, keepdims=True))
    weights = jnp.exp(scores - highest)
    probs = (weights / lax.optimization_barrier(jnp.sum(weights, axis=1, keepdims=True))).astype(jnp.bfloat16)
    latent_out = jnp.dot(probs, cache_block[:, :LATENT], preferred_element_type=jnp.float32).astype(jnp.bfloat16)
    latent_out = latent_out.reshape(DEPTHS * NODES, HEADS, LATENT)
    mixed = jnp.einsum('nhl,hld->nhd', latent_out.astype(jnp.float32), value_up.astype(jnp.float32))
    return mixed.astype(jnp.bfloat16).reshape(DEPTHS, NODES, HEADS * HEAD_DIM)

def reference(node_embed, embed_gain, root_hidden, parents, queries, cache, cache_len, value_up, out_proj, moe_gain, router, expert_ids, w_gate, w_up, w_down):
    heads_all = lax.map(lambda item: attend_request(item[0], item[1], item[2], value_up), (jnp.moveaxis(queries, 1, 0), cache, cache_len))
    heads_all = jnp.moveaxis(heads_all, 0, 1)
    attn_out = jnp.dot(heads_all.reshape(-1, HEADS * HEAD_DIM), out_proj, preferred_element_type=jnp.float32)
    attn_out = attn_out.astype(jnp.bfloat16).reshape(DEPTHS, REQUESTS, NODES, D)
    embed = node_embed.astype(jnp.float32)
    embed_inv = 1.0 / jnp.sqrt(lax.optimization_barrier(jnp.mean(embed * embed, axis=-1, keepdims=True)) + EPS)
    normed = embed * embed_inv * embed_gain
    slot_total = N_DP * CAP
    expert_list = jnp.arange(EXPERTS, dtype=jnp.int32)
    router_wide = router.astype(jnp.float32)
    outputs = []
    previous = jnp.broadcast_to(root_hidden[:, None, :], (REQUESTS, NODES, D))
    for depth in range(DEPTHS):
        if depth > 0:
            previous = jnp.take_along_axis(outputs[-1], parents[depth - 1][:, :, None].astype(jnp.int32), axis=1)
        hidden_state = (normed[depth] + previous.astype(jnp.float32) + attn_out[depth].astype(jnp.float32)).astype(jnp.bfloat16)
        state_rows = hidden_state.reshape(-1, D).astype(jnp.float32)
        inv_rms = 1.0 / jnp.sqrt(lax.optimization_barrier(jnp.mean(state_rows * state_rows, axis=-1, keepdims=True)) + EPS)
        moe_in = (state_rows * inv_rms * moe_gain).astype(jnp.bfloat16)
        logits = jnp.dot(state_rows * moe_gain, router_wide, precision=lax.Precision.HIGHEST) * inv_rms
        chosen_ids = expert_ids[depth].reshape(-1, TOP).astype(jnp.int32)
        chosen = jax.nn.sigmoid(jnp.take_along_axis(logits, chosen_ids, axis=1))
        route_w = chosen / lax.optimization_barrier(jnp.sum(chosen, axis=1, keepdims=True)) * ROUTE_SCALE

        def add_expert(total, expert):
            named = chosen_ids == expert
            weight = lax.optimization_barrier(jnp.sum(jnp.where(named, route_w, 0.0), axis=1))
            used = jnp.any(named, axis=1)
            order = jnp.argsort(1 - used.astype(jnp.int32), stable=True)[:slot_total].astype(jnp.int32)
            picked = moe_in[order]
            gate = jnp.dot(picked, w_gate[expert], preferred_element_type=jnp.float32)
            upward = jnp.dot(picked, w_up[expert], preferred_element_type=jnp.float32)
            activation = (jax.nn.silu(gate) * upward).astype(jnp.bfloat16)
            expert_out = jnp.dot(activation, w_down[expert], preferred_element_type=jnp.float32).astype(jnp.bfloat16)
            scaled = jnp.where(used[order], weight[order], 0.0)[:, None] * expert_out.astype(jnp.float32)
            return (total.at[order].add(scaled), None)
        start_total = jnp.zeros((REQUESTS * NODES, D), jnp.float32)
        moe_out, _ = lax.scan(add_expert, start_total, expert_list)
        outputs.append((state_rows + moe_out).astype(jnp.bfloat16).reshape(REQUESTS, NODES, D))
    return jnp.stack(outputs)
```

```python
import functools

import jax
import jax.numpy as jnp
from jax import lax
from jax.experimental import pallas as pl
from jax.experimental.pallas import tpu as pltpu
from jax.sharding import PartitionSpec as P

EPS = 1e-06
ROUTE_SCALE = 2.5
SLOTS = 4
HALVES = 2
F32 = jnp.float32
BF16 = jnp.bfloat16
VMEM_BYTES = 48 * 1024 * 1024


def iota(shape, dim):
    return lax.broadcasted_iota(jnp.int32, shape, dim)


def split3(value):
    high = value.astype(BF16)
    rest = value - high.astype(F32)
    middle = rest.astype(BF16)
    low = (rest - middle.astype(F32)).astype(BF16)
    return high, middle, low


def pack_matrix(rows, forward):
    shape = (rows, rows)
    packed, mixed = iota(shape, 0 if forward else 1), iota(shape, 1 if forward else 0)
    per_half = rows // HALVES
    half = packed // per_half
    place = packed - half * per_half
    request = place // SLOTS
    source = request * (HALVES * SLOTS) + half * SLOTS + (place - request * SLOTS)
    return (source == mixed).astype(BF16)


def routing(ids, experts):
    nodes, top = ids.shape
    lane = iota((nodes, experts), 1)
    named = jnp.zeros((nodes, experts), F32)
    for route in range(top):
        named = named + (ids[:, route : route + 1] == lane).astype(F32)
    above = (iota((nodes, nodes), 1) < iota((nodes, nodes), 0)).astype(BF16)
    rank = jnp.dot(above, named.astype(BF16), preferred_element_type=F32)
    columns = experts * HALVES * SLOTS
    spread = (iota((experts, columns), 1) // (HALVES * SLOTS) == iota((experts, columns), 0)).astype(BF16)
    order = jnp.dot(((rank + 1.0) * named).astype(BF16), spread, preferred_element_type=F32)
    column = iota((nodes, columns), 1)
    slot = column - (column // SLOTS) * SLOTS
    placed = order == (slot + 1).astype(F32)
    half = (column // SLOTS) - (column // (HALVES * SLOTS)) * HALVES
    return named, spread, placed, half


def combine(rec, state, stats, ids, experts, width):
    nodes = ids.shape[0]
    named, spread, placed, half = routing(ids, experts)
    logits = stats[:, :experts]
    inv_rms = 1.0 / jnp.sqrt(stats[:, experts : experts + 1] / width + EPS)
    chosen = named / (1.0 + jnp.exp(-(logits * inv_rms)))
    weight = chosen / jnp.sum(chosen, axis=1, keepdims=True) * ROUTE_SCALE
    wide = jnp.dot(
        jnp.concatenate(split3(weight), axis=0), spread, preferred_element_type=F32
    )
    zero = jnp.zeros_like(placed, dtype=F32)
    pieces = []
    for h in range(HALVES):
        for piece in range(3):
            part = wide[piece * nodes : (piece + 1) * nodes]
            pieces.append(jnp.where(placed & (half == h), part, zero))
    mixing = jnp.concatenate(pieces, axis=0).astype(BF16)
    mixed = jnp.dot(mixing, rec, preferred_element_type=F32)
    outs = []
    for h in range(HALVES):
        base = h * 3 * nodes
        outs.append(
            mixed[base : base + nodes]
            + mixed[base + nodes : base + 2 * nodes]
            + mixed[base + 2 * nodes : base + 3 * nodes]
        )
    moe_out = jnp.concatenate(outs, axis=1)
    return (state.astype(F32) + moe_out).astype(BF16)


def owner_kernel(first, last, experts, width, copies, *refs):
    refs = list(refs)
    if not first:
        rec = refs.pop(0)[...]
        state_ref = refs.pop(0)
        stats = refs.pop(0)[...]
        for _ in range(3):
            stats = stats + refs.pop(0)[...]
        ids = refs.pop(0)[...]
        if not last:
            parents = refs.pop(0)[...]
    if first:
        root = refs.pop(0)[...]
    if not last:
        normed = refs.pop(0)[...]
        attn = refs.pop(0)[...]
        next_ids = refs.pop(0)[...]
        router = refs.pop(0)
    if not first:
        drafted_ref = refs.pop(0)
        drafted = combine(rec, state_ref[...], stats, ids, experts, width)
        drafted_ref[...] = drafted
    if last:
        return
    out_state, out_stats, outgoing = refs
    if first:
        previous = root.astype(F32)
    else:
        wide = drafted.astype(F32)
        previous = jnp.zeros_like(wide)
        for node in range(wide.shape[0]):
            previous = previous + jnp.where(parents == node, wide[node : node + 1, :], 0.0)
    state = (normed + previous + attn.astype(BF16).astype(F32)).astype(BF16)
    out_state[...] = state
    wide = state.astype(F32)
    square = jnp.sum(wide * wide, axis=1, keepdims=True)
    parts = jnp.dot(state, router[...], preferred_element_type=F32)
    logits = parts[:, :experts] + parts[:, experts : 2 * experts] + parts[:, 2 * experts : 3 * experts]
    pad = jnp.zeros((wide.shape[0], 128 - experts - 1), F32)
    out_stats[...] = jnp.concatenate([logits, square, pad], axis=1)
    _, _, placed, half = routing(next_ids, experts)
    table = jnp.concatenate(
        [(placed & (half == h)).astype(F32) for h in range(HALVES)], axis=0
    ).astype(BF16)
    part = wide.shape[1] // HALVES
    halves = jnp.concatenate(
        [wide[:, h * part : (h + 1) * part] for h in range(HALVES)], axis=0
    ).astype(BF16)
    sent = lax.dot_general(table, halves, (((0,), (0,)), ((), ())), preferred_element_type=F32)
    sent = sent.reshape(experts, HALVES * SLOTS, part).astype(BF16)
    for copy in range(copies):
        outgoing[:, copy] = sent


def owner_call(first, last, experts, width, copies, args, nodes, quarter):
    outs = []
    if not first:
        outs.append(jax.ShapeDtypeStruct((nodes, quarter), BF16))
    if not last:
        outs.append(jax.ShapeDtypeStruct((nodes, quarter), BF16))
        outs.append(jax.ShapeDtypeStruct((nodes, 128), F32))
        outs.append(
            jax.ShapeDtypeStruct((experts, copies, HALVES * SLOTS, quarter // HALVES), BF16)
        )
    return pl.pallas_call(
        functools.partial(owner_kernel, first, last, experts, width, copies),
        out_shape=outs,
        compiler_params=pltpu.CompilerParams(vmem_limit_bytes=VMEM_BYTES),
    )(*args)


def expert_kernel(width, x_ref, gain_ref, gate_ref, up_ref, act_ref, pack, inv, total):
    step = pl.program_id(0)
    sources, quarters, group, part = x_ref.shape
    rows = sources * group

    def block(index):
        return x_ref[:, index].astype(F32).reshape(rows, part)

    row_half = (iota((rows, 1), 0) // SLOTS) - (iota((rows, 1), 0) // group) * HALVES

    @pl.when(step == 0)
    def _():
        pack[...] = pack_matrix(rows, True)
        square = jnp.zeros((rows, part), F32)
        for index in range(quarters):
            value = block(index)
            square = square + value * value
        summed = jnp.broadcast_to(jnp.sum(square, axis=1, keepdims=True), (rows, 128))
        other = jnp.where(
            row_half == 0, pltpu.roll(summed, rows - SLOTS, 0), pltpu.roll(summed, SLOTS, 0)
        )
        inv[...] = 1.0 / jnp.sqrt((summed + other) / width + EPS)
        total[...] = jnp.zeros_like(total)

    gain = gain_ref[step]
    scaled = block(step) * inv[:, :1]
    scaled = (scaled * jnp.where(row_half == 0, gain[0:1, :], gain[1:2, :])).astype(BF16)
    packed = jnp.dot(pack[...], scaled, preferred_element_type=F32).astype(BF16)
    per_half = rows // HALVES
    hidden = gate_ref.shape[1]
    for h in range(HALVES):
        piece = packed[h * per_half : (h + 1) * per_half]
        span = slice(h * part, (h + 1) * part)
        total[:, :hidden] += jnp.dot(piece, gate_ref[span, :], preferred_element_type=F32)
        total[:, hidden:] += jnp.dot(piece, up_ref[span, :], preferred_element_type=F32)

    @pl.when(step == pl.num_programs(0) - 1)
    def _():
        gate = total[:, :hidden]
        act_ref[...] = (gate / (1.0 + jnp.exp(-gate)) * total[:, hidden:]).astype(BF16)


def expert_call(width, x, gain, gate, up):
    sources, quarters, group, part = x.shape
    rows = sources * group
    hidden = gate.shape[1]
    block = gate.shape[0] // quarters
    return pl.pallas_call(
        functools.partial(expert_kernel, width),
        grid=(quarters,),
        in_specs=[
            pl.BlockSpec(x.shape, lambda i: (0, 0, 0, 0)),
            pl.BlockSpec(gain.shape, lambda i: (0, 0, 0)),
            pl.BlockSpec((block, hidden), lambda i: (i, 0)),
            pl.BlockSpec((block, hidden), lambda i: (i, 0)),
        ],
        out_specs=pl.BlockSpec((rows // HALVES, hidden), lambda i: (0, 0)),
        out_shape=jax.ShapeDtypeStruct((rows // HALVES, hidden), BF16),
        scratch_shapes=[
            pltpu.VMEM((rows, rows), BF16),
            pltpu.VMEM((rows, 128), F32),
            pltpu.VMEM((rows // HALVES, 2 * hidden), F32),
        ],
        compiler_params=pltpu.CompilerParams(vmem_limit_bytes=VMEM_BYTES),
    )(x, gain, gate, up)


def down_kernel(count, *refs):
    acts, weights, out_ref = refs[:count], refs[count : 2 * count], refs[2 * count]
    total = jnp.dot(acts[0][...], weights[0][...], preferred_element_type=F32)
    for index in range(1, count):
        total = total + jnp.dot(acts[index][...], weights[index][...], preferred_element_type=F32)
    part = total.shape[1] // HALVES
    stacked = jnp.concatenate(
        [total[:, h * part : (h + 1) * part] for h in range(HALVES)], axis=0
    ).astype(BF16)
    unpack = pack_matrix(stacked.shape[0], False)
    out_ref[...] = jnp.dot(unpack, stacked, preferred_element_type=F32).astype(BF16)


def down_call(acts, weights):
    rows = acts[0].shape[0]
    quarter = weights[0].shape[1]
    return pl.pallas_call(
        functools.partial(down_kernel, len(acts)),
        out_shape=jax.ShapeDtypeStruct((rows * HALVES, quarter // HALVES), BF16),
        compiler_params=pltpu.CompilerParams(vmem_limit_bytes=VMEM_BYTES),
    )(*acts, *weights)


def attend_request(query_block, cache_block, length, value_up, score_scale):
    depths, nodes, heads_dev, width_qk = query_block.shape
    latent = value_up.shape[1]
    query_rows = query_block.reshape(-1, width_qk)
    scores = (
        jnp.einsum("qk,ck->qc", query_rows, cache_block, preferred_element_type=F32)
        * score_scale
    )
    valid = jnp.arange(cache_block.shape[0], dtype=jnp.int32) < length
    scores = jnp.where(valid[None, :], scores, -jnp.inf)
    highest = jnp.max(scores, axis=1, keepdims=True)
    weights = jnp.exp(scores - highest)
    probs = (weights / jnp.sum(weights, axis=1, keepdims=True)).astype(BF16)
    latent_out = jnp.dot(probs, cache_block[:, :latent], preferred_element_type=F32).astype(BF16)
    latent_out = latent_out.reshape(depths * nodes, heads_dev, latent)
    mixed = jnp.einsum("nhl,hld->nhd", latent_out, value_up, preferred_element_type=F32)
    return mixed.astype(BF16).reshape(depths, nodes, -1)


def local(
    node_embed,
    embed_gain,
    root_hidden,
    parents,
    queries,
    cache,
    cache_len,
    value_up,
    out_proj,
    moe_gain,
    router,
    expert_ids,
    w_gate,
    w_up,
    w_down,
):
    depths, _, nodes, quarter = node_embed.shape
    groups = lax.axis_size("dp")
    tp = lax.axis_size("tp")
    mine = lax.axis_index("tp")
    width = quarter * tp
    part = quarter // HALVES
    experts = router.shape[1]
    latent = value_up.shape[1]
    score_scale = (value_up.shape[2] + cache.shape[2] - latent) ** (-0.5)
    shifts = {k: [(i, (i + k) % tp) for i in range(tp)] for k in range(1, tp)}

    def share(value):
        return [value] + [lax.ppermute(value, "tp", shifts[k]) for k in range(1, tp)]

    def deal(pick):
        return [pick(mine)] + [
            lax.ppermute(pick((mine + k) % tp), "tp", shifts[k]) for k in range(1, tp)
        ]

    down = deal(lambda i: lax.dynamic_slice(w_down[0], (0, i * quarter), (w_down.shape[1], quarter)))
    embed = node_embed[:, 0].astype(F32)
    embed_sq = sum(share(jnp.sum(embed * embed, axis=-1)))
    normed = embed * (1.0 / jnp.sqrt(embed_sq / width + EPS))[..., None] * embed_gain
    gains = jnp.stack(share(moe_gain.reshape(HALVES, part)))
    gains = gains[(mine - jnp.arange(tp, dtype=jnp.int32)) % tp]
    product = router.astype(F32) * moe_gain[:, None]
    high = lax.reduce_precision(product, 8, 7)
    middle = lax.reduce_precision(product - high, 8, 7)
    low = product - high - middle
    routed = jnp.concatenate(
        [high, middle, low, jnp.zeros((quarter, 128 - 3 * experts), F32)], axis=1
    ).astype(BF16)

    heads_all = attend_request(queries[:, 0], cache[0], cache_len[0], value_up, score_scale)

    def attention_out(depth):
        rows = lax.all_gather(heads_all[depth], "dp", axis=0, tiled=True)
        columns = jnp.dot(rows, out_proj, preferred_element_type=F32).astype(BF16)
        columns = columns.reshape(groups, nodes, -1)
        columns = lax.all_to_all(columns, "dp", split_axis=0, concat_axis=0, tiled=True)
        columns = columns.reshape(tp, groups // tp, nodes, columns.shape[2])
        pieces = deal(lambda i: lax.dynamic_index_in_dim(columns, i, 0, keepdims=False))
        summed = sum(piece.astype(F32) for piece in pieces)
        return jnp.moveaxis(summed, 0, 1).reshape(nodes, quarter)

    attn = [attention_out(depth) for depth in range(depths)]

    drafted = []
    carried = None
    for depth in range(depths + 1):
        first, last = depth == 0, depth == depths
        args = []
        if not first:
            args += list(carried) + [expert_ids[depth - 1, 0]]
            if not last:
                args += [parents[depth - 1, 0][:, None]]
        if first:
            args += [root_hidden]
        if not last:
            args += [normed[depth], attn[depth], expert_ids[depth, 0], routed]
        result = list(owner_call(first, last, experts, width, tp, args, nodes, quarter))
        if not first:
            drafted.append(result.pop(0))
        if last:
            break
        state, stats, outgoing = result
        all_stats = share(stats)
        outgoing = outgoing.reshape(experts * tp, HALVES * SLOTS, part)
        arrived = lax.all_to_all(outgoing, ("dp", "tp"), split_axis=0, concat_axis=0, tiled=True)
        arrived = arrived.reshape(groups, tp, HALVES * SLOTS, part)
        act = expert_call(width, arrived, gains, w_gate[0], w_up[0])
        answer = down_call(share(act), down)
        answer = answer.reshape(groups, HALVES * SLOTS, part)
        returned = lax.all_to_all(answer, "dp", split_axis=0, concat_axis=0, tiled=True)
        carried = [returned.reshape(groups * HALVES * SLOTS, part), state] + all_stats
    return jnp.stack(drafted)[:, None]


def solution(mesh):
    placed = (
        P(None, "dp", None, "tp"),
        P("tp"),
        P("dp", "tp"),
        P(None, "dp", None),
        P(None, "dp", None, "tp", None),
        P("dp", None, None),
        P("dp"),
        P("tp", None, None),
        P("tp", "dp"),
        P("tp"),
        P("tp", None),
        P(None, "dp", None, None),
        P("dp", None, "tp"),
        P("dp", None, "tp"),
        P("dp", "tp", None),
    )
    return jax.shard_map(
        local, mesh=mesh, in_specs=placed, out_specs=P(None, "dp", None, "tp"), check_vma=False
    )
```

```python
import functools

import jax
import jax.numpy as jnp
from jax import lax
from jax.experimental import pallas as pl
from jax.experimental.pallas import tpu as pltpu
from jax.sharding import PartitionSpec as P

EPS = 1e-06
ROUTE_SCALE = 2.5
SLOTS = 4
HALVES = 2
F32 = jnp.float32
BF16 = jnp.bfloat16
VMEM_BYTES = 48 * 1024 * 1024


def iota(shape, dim):
    return lax.broadcasted_iota(jnp.int32, shape, dim)


def split3(value):
    high = value.astype(BF16)
    rest = value - high.astype(F32)
    middle = rest.astype(BF16)
    low = (rest - middle.astype(F32)).astype(BF16)
    return high, middle, low


def pack_matrix(rows, forward):
    shape = (rows, rows)
    packed, mixed = iota(shape, 0 if forward else 1), iota(shape, 1 if forward else 0)
    per_half = rows // HALVES
    half = packed // per_half
    place = packed - half * per_half
    request = place // SLOTS
    source = request * (HALVES * SLOTS) + half * SLOTS + (place - request * SLOTS)
    return (source == mixed).astype(BF16)


def routing(ids, experts):
    nodes, top = ids.shape
    lane = iota((nodes, experts), 1)
    named = jnp.zeros((nodes, experts), F32)
    for route in range(top):
        named = named + (ids[:, route : route + 1] == lane).astype(F32)
    above = (iota((nodes, nodes), 1) < iota((nodes, nodes), 0)).astype(BF16)
    rank = jnp.dot(above, named.astype(BF16), preferred_element_type=F32)
    columns = experts * HALVES * SLOTS
    spread = (iota((experts, columns), 1) // (HALVES * SLOTS) == iota((experts, columns), 0)).astype(BF16)
    order = jnp.dot(((rank + 1.0) * named).astype(BF16), spread, preferred_element_type=F32)
    column = iota((nodes, columns), 1)
    slot = column - (column // SLOTS) * SLOTS
    placed = order == (slot + 1).astype(F32)
    half = (column // SLOTS) - (column // (HALVES * SLOTS)) * HALVES
    return named, spread, placed, half


def combine(rec, state, stats, ids, experts, width):
    nodes = ids.shape[0]
    named, spread, placed, half = routing(ids, experts)
    logits = stats[:, :experts]
    inv_rms = 1.0 / jnp.sqrt(stats[:, experts : experts + 1] / width + EPS)
    chosen = named / (1.0 + jnp.exp(-(logits * inv_rms)))
    weight = chosen / jnp.sum(chosen, axis=1, keepdims=True) * ROUTE_SCALE
    wide = jnp.dot(
        jnp.concatenate(split3(weight), axis=0), spread, preferred_element_type=F32
    )
    zero = jnp.zeros_like(placed, dtype=F32)
    pieces = []
    for h in range(HALVES):
        for piece in range(3):
            part = wide[piece * nodes : (piece + 1) * nodes]
            pieces.append(jnp.where(placed & (half == h), part, zero))
    mixing = jnp.concatenate(pieces, axis=0).astype(BF16)
    mixed = jnp.dot(mixing, rec, preferred_element_type=F32)
    outs = []
    for h in range(HALVES):
        base = h * 3 * nodes
        outs.append(
            mixed[base : base + nodes]
            + mixed[base + nodes : base + 2 * nodes]
            + mixed[base + 2 * nodes : base + 3 * nodes]
        )
    moe_out = jnp.concatenate(outs, axis=1)
    return (state.astype(F32) + moe_out).astype(BF16)


def owner_kernel(depth, depths, experts, width, copies, *refs):
    first, last = depth == 0, depth == depths
    refs = list(refs)
    ids_ref = refs.pop(0)
    if first:
        root = refs.pop(0)[...]
        base = refs.pop(0)[...]
        attn = refs.pop(0)[...].astype(F32)
        for _ in range(3):
            attn = attn + refs.pop(0)[...].astype(F32)
        base = base + attn.astype(BF16).astype(F32).reshape(base.shape)
    else:
        rec = refs.pop(0)[...]
        state_ref = refs.pop(0)
        stats = refs.pop(0)[...]
        for _ in range(3):
            stats = stats + refs.pop(0)[...]
    if not last:
        router = refs.pop(0)[...]
        gain = refs.pop(0)[...]
    if not first and not last:
        parents = refs.pop(0)[depth - 1]
        base_ref = refs.pop(0)
    if not first:
        drafted_ref = refs.pop(0)
        drafted = combine(rec, state_ref[...], stats, ids_ref[depth - 1], experts, width)
        drafted_ref[...] = drafted
    if last:
        return
    out_state, out_stats, outgoing = refs[:3]
    if first:
        refs[3][...] = base[1:]
        start = base[0]
        previous = root.astype(F32)
    else:
        start = base_ref[depth - 1]
        wide = drafted.astype(F32)
        previous = jnp.zeros_like(wide)
        for node in range(wide.shape[0]):
            previous = previous + jnp.where(parents == node, wide[node : node + 1, :], 0.0)
    state = (start + previous).astype(BF16)
    out_state[...] = state
    wide = state.astype(F32)
    square = jnp.sum(wide * wide, axis=1, keepdims=True)
    product = split3(router.astype(F32) * gain)
    contract = (((1,), (1,)), ((), ()))
    logits = lax.dot_general(state, product[0], contract, preferred_element_type=F32)
    for piece in product[1:]:
        logits = logits + lax.dot_general(state, piece, contract, preferred_element_type=F32)
    pad = jnp.zeros((wide.shape[0], 128 - experts - 1), F32)
    out_stats[...] = jnp.concatenate([logits, square, pad], axis=1)
    _, _, placed, half = routing(ids_ref[depth], experts)
    table = jnp.concatenate(
        [(placed & (half == h)).astype(F32) for h in range(HALVES)], axis=0
    ).astype(BF16)
    part = wide.shape[1] // HALVES
    halves = jnp.concatenate(
        [wide[:, h * part : (h + 1) * part] for h in range(HALVES)], axis=0
    ).astype(BF16)
    sent = lax.dot_general(table, halves, (((0,), (0,)), ((), ())), preferred_element_type=F32)
    sent = sent.reshape(experts, HALVES * SLOTS, part).astype(BF16)
    for copy in range(copies):
        outgoing[:, copy] = sent


def owner_call(depth, depths, experts, width, copies, args, nodes, quarter):
    outs = []
    if depth > 0:
        outs.append(jax.ShapeDtypeStruct((nodes, quarter), BF16))
    if depth < depths:
        outs.append(jax.ShapeDtypeStruct((nodes, quarter), BF16))
        outs.append(jax.ShapeDtypeStruct((nodes, 128), F32))
        outs.append(
            jax.ShapeDtypeStruct((experts, copies, HALVES * SLOTS, quarter // HALVES), BF16)
        )
    if depth == 0:
        outs.append(jax.ShapeDtypeStruct((depths - 1, nodes, quarter), F32))
    return pl.pallas_call(
        functools.partial(owner_kernel, depth, depths, experts, width, copies),
        out_shape=outs,
        compiler_params=pltpu.CompilerParams(vmem_limit_bytes=VMEM_BYTES),
    )(*args)


def expert_kernel(width, x_ref, gain_ref, gate_ref, up_ref, act_ref, pack, inv, total):
    step = pl.program_id(0)
    sources, quarters, group, part = x_ref.shape
    rows = sources * group

    def block(index):
        return x_ref[:, index].astype(F32).reshape(rows, part)

    row_half = (iota((rows, 1), 0) // SLOTS) - (iota((rows, 1), 0) // group) * HALVES

    @pl.when(step == 0)
    def _():
        pack[...] = pack_matrix(rows, True)
        square = jnp.zeros((rows, part), F32)
        for index in range(quarters):
            value = block(index)
            square = square + value * value
        summed = jnp.broadcast_to(jnp.sum(square, axis=1, keepdims=True), (rows, 128))
        other = jnp.where(
            row_half == 0, pltpu.roll(summed, rows - SLOTS, 0), pltpu.roll(summed, SLOTS, 0)
        )
        inv[...] = 1.0 / jnp.sqrt((summed + other) / width + EPS)
        total[...] = jnp.zeros_like(total)

    gain = gain_ref[step]
    scaled = block(step) * inv[:, :1]
    scaled = (scaled * jnp.where(row_half == 0, gain[0:1, :], gain[1:2, :])).astype(BF16)
    packed = jnp.dot(pack[...], scaled, preferred_element_type=F32).astype(BF16)
    per_half = rows // HALVES
    hidden = gate_ref.shape[1]
    for h in range(HALVES):
        piece = packed[h * per_half : (h + 1) * per_half]
        span = slice(h * part, (h + 1) * part)
        total[:, :hidden] += jnp.dot(piece, gate_ref[span, :], preferred_element_type=F32)
        total[:, hidden:] += jnp.dot(piece, up_ref[span, :], preferred_element_type=F32)

    @pl.when(step == pl.num_programs(0) - 1)
    def _():
        gate = total[:, :hidden]
        act_ref[...] = (gate / (1.0 + jnp.exp(-gate)) * total[:, hidden:]).astype(BF16)


def expert_call(width, x, gain, gate, up):
    sources, quarters, group, part = x.shape
    rows = sources * group
    hidden = gate.shape[1]
    block = gate.shape[0] // quarters
    return pl.pallas_call(
        functools.partial(expert_kernel, width),
        grid=(quarters,),
        in_specs=[
            pl.BlockSpec(x.shape, lambda i: (0, 0, 0, 0)),
            pl.BlockSpec(gain.shape, lambda i: (0, 0, 0)),
            pl.BlockSpec((block, hidden), lambda i: (i, 0)),
            pl.BlockSpec((block, hidden), lambda i: (i, 0)),
        ],
        out_specs=pl.BlockSpec((rows // HALVES, hidden), lambda i: (0, 0)),
        out_shape=jax.ShapeDtypeStruct((rows // HALVES, hidden), BF16),
        scratch_shapes=[
            pltpu.VMEM((rows, rows), BF16),
            pltpu.VMEM((rows, 128), F32),
            pltpu.VMEM((rows // HALVES, 2 * hidden), F32),
        ],
        compiler_params=pltpu.CompilerParams(vmem_limit_bytes=VMEM_BYTES),
    )(x, gain, gate, up)


def down_kernel(count, *refs):
    acts, weights, out_ref = refs[:count], refs[count : 2 * count], refs[2 * count]
    total = jnp.dot(acts[0][...], weights[0][...], preferred_element_type=F32)
    for index in range(1, count):
        total = total + jnp.dot(acts[index][...], weights[index][...], preferred_element_type=F32)
    part = total.shape[1] // HALVES
    stacked = jnp.concatenate(
        [total[:, h * part : (h + 1) * part] for h in range(HALVES)], axis=0
    ).astype(BF16)
    unpack = pack_matrix(stacked.shape[0], False)
    out_ref[...] = jnp.dot(unpack, stacked, preferred_element_type=F32).astype(BF16)


def down_call(acts, weights):
    rows = acts[0].shape[0]
    quarter = weights[0].shape[1]
    return pl.pallas_call(
        functools.partial(down_kernel, len(acts)),
        out_shape=jax.ShapeDtypeStruct((rows * HALVES, quarter // HALVES), BF16),
        compiler_params=pltpu.CompilerParams(vmem_limit_bytes=VMEM_BYTES),
    )(*acts, *weights)


def project_kernel(rows_ref, weight_ref, out_ref):
    columns = lax.dot_general(
        rows_ref[...], weight_ref[...], (((1,), (1,)), ((), ())), preferred_element_type=F32
    )
    out_ref[...] = columns.reshape(out_ref.shape).astype(BF16)


def project(rows, weight, owners):
    steps = 4
    group = rows.shape[0] // owners
    return pl.pallas_call(
        project_kernel,
        grid=(steps,),
        in_specs=[
            pl.BlockSpec((rows.shape[0] // steps, rows.shape[1]), lambda i: (i, 0)),
            pl.BlockSpec(weight.shape, lambda i: (0, 0)),
        ],
        out_specs=pl.BlockSpec((owners // steps, group, weight.shape[0]), lambda i: (i, 0, 0)),
        out_shape=jax.ShapeDtypeStruct((owners, group, weight.shape[0]), BF16),
        compiler_params=pltpu.CompilerParams(vmem_limit_bytes=VMEM_BYTES),
    )(rows, weight)


def settle_kernel(place_ref, x_ref, *refs):
    outs, wide = refs[:-1], refs[-1]
    quarters = len(outs)
    blocks, _, columns = x_ref.shape
    value = x_ref[...].astype(F32)
    per = blocks // quarters
    for block in range(blocks):
        at = (block % per) * columns
        wide[block // per, :, at : at + columns] = value[block]
    for k in range(quarters):
        outs[k][...] = wide[lax.rem(place_ref[0] + k, quarters)].astype(BF16)


def settle(place, x, quarters):
    blocks, rows, columns = x.shape
    width = blocks // quarters * columns
    return pl.pallas_call(
        settle_kernel,
        in_specs=[
            pl.BlockSpec(memory_space=pltpu.SMEM),
            pl.BlockSpec(memory_space=pltpu.VMEM),
        ],
        out_shape=[jax.ShapeDtypeStruct((rows, width), BF16) for _ in range(quarters)],
        scratch_shapes=[pltpu.VMEM((quarters, rows, width), F32)],
        compiler_params=pltpu.CompilerParams(vmem_limit_bytes=VMEM_BYTES),
    )(place, x)


def attend_request(query_block, cache_block, length, value_up, score_scale):
    depths, nodes, heads_dev, width_qk = query_block.shape
    latent = value_up.shape[1]
    query_rows = query_block.reshape(-1, width_qk)
    scores = (
        jnp.einsum("qk,ck->qc", query_rows, cache_block, preferred_element_type=F32)
        * score_scale
    )
    valid = jnp.arange(cache_block.shape[0], dtype=jnp.int32) < length
    scores = jnp.where(valid[None, :], scores, -jnp.inf)
    highest = jnp.max(scores, axis=1, keepdims=True)
    weights = jnp.exp(scores - highest)
    probs = (weights / jnp.sum(weights, axis=1, keepdims=True)).astype(BF16)
    latent_out = jnp.dot(probs, cache_block[:, :latent], preferred_element_type=F32).astype(BF16)
    latent_out = latent_out.reshape(depths * nodes, heads_dev, latent)
    mixed = jnp.einsum("nhl,hld->nhd", latent_out, value_up, preferred_element_type=F32)
    return mixed.astype(BF16).reshape(depths, nodes, -1)


def local(
    node_embed,
    embed_gain,
    root_hidden,
    parents,
    queries,
    cache,
    cache_len,
    value_up,
    out_proj,
    moe_gain,
    router,
    expert_ids,
    w_gate,
    w_up,
    w_down,
):
    depths, _, nodes, quarter = node_embed.shape
    groups = lax.axis_size("dp")
    tp = lax.axis_size("tp")
    mine = lax.axis_index("tp")
    width = quarter * tp
    part = quarter // HALVES
    experts = router.shape[1]
    latent = value_up.shape[1]
    score_scale = (value_up.shape[2] + cache.shape[2] - latent) ** (-0.5)
    shifts = {k: [(i, (i + k) % tp) for i in range(tp)] for k in range(1, tp)}

    def share(value):
        return [value] + [lax.ppermute(value, "tp", shifts[k]) for k in range(1, tp)]

    def deal(values):
        return [values[0]] + [lax.ppermute(values[k], "tp", shifts[k]) for k in range(1, tp)]

    heads = attend_request(queries[:, 0], cache[0], cache_len[0], value_up, score_scale)
    heads = heads.reshape(depths * nodes, -1)
    gathered = lax.all_gather(heads, "dp", axis=0, tiled=True)

    w_down, node_embed, heads = lax.optimization_barrier((w_down, node_embed, heads))
    down = deal(
        [
            lax.dynamic_slice(
                w_down[0], (0, (mine + k) % tp * quarter), (w_down.shape[1], quarter)
            )
            for k in range(tp)
        ]
    )
    embed = node_embed[:, 0].astype(F32)
    squares = jnp.sum(embed * embed, axis=-1).reshape(1, depths * nodes)
    gain_rows = quarter // 128
    notes = jnp.concatenate(
        [
            moe_gain.reshape(gain_rows, 128),
            jnp.pad(squares, ((0, 1), (0, 128 - depths * nodes))),
        ]
    )
    notes = jnp.stack(share(notes))
    embed_sq = jnp.sum(notes[:, gain_rows, : depths * nodes], axis=0).reshape(depths, nodes)
    normed = embed * (1.0 / jnp.sqrt(embed_sq / width + EPS))[..., None] * embed_gain
    gains = notes[(mine - jnp.arange(tp, dtype=jnp.int32)) % tp, :gain_rows].reshape(tp, HALVES, part)
    gathered, normed, gains, *down = lax.optimization_barrier((gathered, normed, gains, *down))

    columns = project(gathered, out_proj.T, groups)
    columns = lax.all_to_all(columns, "dp", split_axis=0, concat_axis=0, tiled=True)
    attn = deal(settle(mine.reshape(1).astype(jnp.int32), columns, tp))

    drafted = []
    carried = None
    ids = expert_ids[:, 0]
    parent_columns = parents[:, 0, :, None]
    for depth in range(depths + 1):
        args = [ids]
        args += [root_hidden, normed, *attn] if depth == 0 else carried
        if depth < depths:
            args += [router.T, moe_gain[None]]
        if 0 < depth < depths:
            args += [parent_columns, base]
        result = list(owner_call(depth, depths, experts, width, tp, args, nodes, quarter))
        if depth > 0:
            drafted.append(result.pop(0))
        if depth == depths:
            break
        if depth == 0:
            base = result.pop()
        state, stats, outgoing = result
        all_stats = share(stats)
        outgoing = outgoing.reshape(experts * tp, HALVES * SLOTS, part)
        arrived = lax.all_to_all(outgoing, ("dp", "tp"), split_axis=0, concat_axis=0, tiled=True)
        arrived = arrived.reshape(groups, tp, HALVES * SLOTS, part)
        act = expert_call(width, arrived, gains, w_gate[0], w_up[0])
        answer = down_call(share(act), down)
        answer = answer.reshape(groups, HALVES * SLOTS, part)
        returned = lax.all_to_all(answer, "dp", split_axis=0, concat_axis=0, tiled=True)
        carried = [returned.reshape(groups * HALVES * SLOTS, part), state] + all_stats
    return jnp.stack(drafted)[:, None]


def solution(mesh):
    placed = (
        P(None, "dp", None, "tp"),
        P("tp"),
        P("dp", "tp"),
        P(None, "dp", None),
        P(None, "dp", None, "tp", None),
        P("dp", None, None),
        P("dp"),
        P("tp", None, None),
        P("tp", "dp"),
        P("tp"),
        P("tp", None),
        P(None, "dp", None, None),
        P("dp", None, "tp"),
        P("dp", None, "tp"),
        P("dp", "tp", None),
    )
    return jax.shard_map(
        local, mesh=mesh, in_specs=placed, out_specs=P(None, "dp", None, "tp"), check_vma=False
    )
```

```python
import functools
import math

import jax
import jax.numpy as jnp
from jax import lax
from jax.experimental import pallas as pl
from jax.experimental.pallas import tpu as pltpu
from jax.sharding import PartitionSpec as P

EPS = 1e-06
ROUTE_SCALE = 2.5
SLOTS = 4
HALVES = 2
F32 = jnp.float32
BF16 = jnp.bfloat16
VMEM_BYTES = 48 * 1024 * 1024


def iota(shape, dim):
    return lax.broadcasted_iota(jnp.int32, shape, dim)


def split3(value):
    high = value.astype(BF16)
    rest = value - high.astype(F32)
    middle = rest.astype(BF16)
    low = (rest - middle.astype(F32)).astype(BF16)
    return high, middle, low


def pack_matrix(rows, forward):
    shape = (rows, rows)
    packed, mixed = iota(shape, 0 if forward else 1), iota(shape, 1 if forward else 0)
    per_half = rows // HALVES
    half = packed // per_half
    place = packed - half * per_half
    request = place // SLOTS
    source = request * (HALVES * SLOTS) + half * SLOTS + (place - request * SLOTS)
    return (source == mixed).astype(BF16)


def routing(ids, experts):
    nodes, top = ids.shape
    lane = iota((nodes, experts), 1)
    named = jnp.zeros((nodes, experts), F32)
    for route in range(top):
        named = named + (ids[:, route : route + 1] == lane).astype(F32)
    above = (iota((nodes, nodes), 1) < iota((nodes, nodes), 0)).astype(BF16)
    rank = jnp.dot(above, named.astype(BF16), preferred_element_type=F32)
    columns = experts * HALVES * SLOTS
    spread = (iota((experts, columns), 1) // (HALVES * SLOTS) == iota((experts, columns), 0)).astype(BF16)
    order = jnp.dot(((rank + 1.0) * named).astype(BF16), spread, preferred_element_type=F32)
    column = iota((nodes, columns), 1)
    slot = column - (column // SLOTS) * SLOTS
    placed = order == (slot + 1).astype(F32)
    half = (column // SLOTS) - (column // (HALVES * SLOTS)) * HALVES
    return named, spread, placed, half


def combine(rec, state, stats, ids, experts, width):
    nodes = ids.shape[0]
    named, spread, placed, half = routing(ids, experts)
    logits = stats[:, :experts]
    inv_rms = 1.0 / jnp.sqrt(stats[:, experts : experts + 1] / width + EPS)
    chosen = named / (1.0 + jnp.exp(-(logits * inv_rms)))
    weight = chosen / jnp.sum(chosen, axis=1, keepdims=True) * ROUTE_SCALE
    wide = jnp.dot(
        jnp.concatenate(split3(weight), axis=0), spread, preferred_element_type=F32
    )
    zero = jnp.zeros_like(placed, dtype=F32)
    pieces = []
    for h in range(HALVES):
        for piece in range(3):
            part = wide[piece * nodes : (piece + 1) * nodes]
            pieces.append(jnp.where(placed & (half == h), part, zero))
    mixing = jnp.concatenate(pieces, axis=0).astype(BF16)
    mixed = jnp.dot(mixing, rec, preferred_element_type=F32)
    outs = []
    for h in range(HALVES):
        base = h * 3 * nodes
        outs.append(
            mixed[base : base + nodes]
            + mixed[base + nodes : base + 2 * nodes]
            + mixed[base + 2 * nodes : base + 3 * nodes]
        )
    moe_out = jnp.concatenate(outs, axis=1)
    return (state.astype(F32) + moe_out).astype(BF16)


def owner_kernel(depth, depths, experts, width, copies, *refs):
    first, last = depth == 0, depth == depths
    refs = list(refs)
    tables = refs.pop(0)
    top = tables.shape[2] - 1
    if first:
        root = refs.pop(0)[...]
        start = refs.pop(0)[...]
        attn = refs.pop(0)[...].astype(F32)
        for _ in range(3):
            attn = attn + refs.pop(0)[...].astype(F32)
        start = start + attn.astype(BF16).astype(F32).reshape(start.shape)
        base, start = start[1:], start[0]
        router = refs.pop(0)[...].astype(F32)
        product = split3(router * refs.pop(0)[...])
        blank = jnp.zeros((128 - 3 * experts, router.shape[1]), BF16)
        routed = jnp.concatenate([*product, blank], axis=0)
    else:
        rec = refs.pop(0)[...]
        state_ref = refs.pop(0)
        stats = refs.pop(0)[...]
        for _ in range(3):
            stats = stats + refs.pop(0)[...]
    if not first and not last:
        routed = refs.pop(0)[...]
        start = refs.pop(0)[depth - 1]
    if not first:
        drafted_ref = refs.pop(0)
        drafted = combine(rec, state_ref[...], stats, tables[depth - 1][:, :top], experts, width)
        drafted_ref[...] = drafted
    if last:
        return
    out_state, out_stats, outgoing = refs[:3]
    if first:
        refs[3][...] = routed
        refs[4][...] = base
        previous = root.astype(F32)
    else:
        parents = tables[depth][:, top : top + 1]
        wide = drafted.astype(F32)
        previous = jnp.zeros_like(wide)
        for node in range(wide.shape[0]):
            previous = previous + jnp.where(parents == node, wide[node : node + 1, :], 0.0)
    state = (start + previous).astype(BF16)
    out_state[...] = state
    wide = state.astype(F32)
    square = jnp.sum(wide * wide, axis=1, keepdims=True)
    parts = lax.dot_general(
        state, routed, (((1,), (1,)), ((), ())), preferred_element_type=F32
    )
    logits = parts[:, :experts] + parts[:, experts : 2 * experts] + parts[:, 2 * experts : 3 * experts]
    pad = jnp.zeros((wide.shape[0], 128 - experts - 1), F32)
    out_stats[...] = jnp.concatenate([logits, square, pad], axis=1)
    _, _, placed, half = routing(tables[depth][:, :top], experts)
    table = jnp.concatenate(
        [(placed & (half == h)).astype(F32) for h in range(HALVES)], axis=0
    ).astype(BF16)
    part = wide.shape[1] // HALVES
    halves = jnp.concatenate(
        [wide[:, h * part : (h + 1) * part] for h in range(HALVES)], axis=0
    ).astype(BF16)
    sent = lax.dot_general(table, halves, (((0,), (0,)), ((), ())), preferred_element_type=F32)
    sent = sent.reshape(experts, HALVES * SLOTS, part).astype(BF16)
    for copy in range(copies):
        outgoing[:, copy] = sent


def owner_call(depth, depths, experts, width, copies, args, nodes, quarter):
    outs = []
    if depth > 0:
        outs.append(jax.ShapeDtypeStruct((nodes, quarter), BF16))
    if depth < depths:
        outs.append(jax.ShapeDtypeStruct((nodes, quarter), BF16))
        outs.append(jax.ShapeDtypeStruct((nodes, 128), F32))
        outs.append(
            jax.ShapeDtypeStruct((experts, copies, HALVES * SLOTS, quarter // HALVES), BF16)
        )
    if depth == 0:
        outs.append(jax.ShapeDtypeStruct((128, quarter), BF16))
        outs.append(jax.ShapeDtypeStruct((depths - 1, nodes, quarter), F32))
    return pl.pallas_call(
        functools.partial(owner_kernel, depth, depths, experts, width, copies),
        out_shape=outs,
        compiler_params=pltpu.CompilerParams(vmem_limit_bytes=VMEM_BYTES),
    )(*args)


def expert_kernel(width, x_ref, gain_ref, gate_ref, up_ref, act_ref, pack, square, total):
    step = pl.program_id(0)
    sources, _, group, part = x_ref.shape
    rows = sources * group
    per_half = rows // HALVES
    hidden = gate_ref.shape[1]

    @pl.when(step == 0)
    def _():
        pack[...] = pack_matrix(rows, True)
        square[...] = jnp.zeros_like(square)
        total[...] = jnp.zeros_like(total)

    mixed = x_ref[:, step].astype(F32).reshape(rows, part).astype(BF16)
    packed = jnp.dot(pack[...], mixed, preferred_element_type=F32)
    gain = gain_ref[step]
    for h in range(HALVES):
        piece = packed[h * per_half : (h + 1) * per_half]
        square[...] += jnp.sum(piece * piece, axis=1, keepdims=True)
        piece = (piece * gain[h : h + 1, :]).astype(BF16)
        span = slice(h * part, (h + 1) * part)
        total[:, :hidden] += jnp.dot(piece, gate_ref[span, :], preferred_element_type=F32)
        total[:, hidden:] += jnp.dot(piece, up_ref[span, :], preferred_element_type=F32)

    @pl.when(step == pl.num_programs(0) - 1)
    def _():
        inv = 1.0 / jnp.sqrt(square[...] / width + EPS)
        gate = total[:, :hidden] * inv
        act_ref[...] = (gate / (1.0 + jnp.exp(-gate)) * (total[:, hidden:] * inv)).astype(BF16)


def expert_call(width, x, gain, gate, up):
    sources, quarters, group, part = x.shape
    rows = sources * group
    hidden = gate.shape[1]
    block = gate.shape[0] // quarters
    return pl.pallas_call(
        functools.partial(expert_kernel, width),
        grid=(quarters,),
        in_specs=[
            pl.BlockSpec(x.shape, lambda i: (0, 0, 0, 0)),
            pl.BlockSpec(gain.shape, lambda i: (0, 0, 0)),
            pl.BlockSpec((block, hidden), lambda i: (i, 0)),
            pl.BlockSpec((block, hidden), lambda i: (i, 0)),
        ],
        out_specs=pl.BlockSpec((rows // HALVES, hidden), lambda i: (0, 0)),
        out_shape=jax.ShapeDtypeStruct((rows // HALVES, hidden), BF16),
        scratch_shapes=[
            pltpu.VMEM((rows, rows), BF16),
            pltpu.VMEM((rows // HALVES, 1), F32),
            pltpu.VMEM((rows // HALVES, 2 * hidden), F32),
        ],
        compiler_params=pltpu.CompilerParams(vmem_limit_bytes=VMEM_BYTES),
    )(x, gain, gate, up)


def down_kernel(count, *refs):
    acts, weights, out_ref, stacked = refs[:count], refs[count : 2 * count], *refs[2 * count :]
    step = pl.program_id(0)
    total = jnp.dot(acts[0][...], weights[0][...], preferred_element_type=F32)
    for index in range(1, count):
        total = total + jnp.dot(acts[index][...], weights[index][...], preferred_element_type=F32)
    stacked[step] = total.astype(BF16)

    @pl.when(step == HALVES - 1)
    def _():
        rows, part = out_ref.shape
        unpack = pack_matrix(rows, False)
        value = stacked[...].reshape(rows, part)
        out_ref[...] = jnp.dot(unpack, value, preferred_element_type=F32).astype(BF16)


def down_call(acts, weights):
    rows = acts[0].shape[0]
    hidden, quarter = weights[0].shape
    part = quarter // HALVES
    return pl.pallas_call(
        functools.partial(down_kernel, len(acts)),
        grid=(HALVES,),
        in_specs=[pl.BlockSpec(acts[0].shape, lambda i: (0, 0)) for _ in acts]
        + [pl.BlockSpec((hidden, part), lambda i: (0, i)) for _ in weights],
        out_specs=pl.BlockSpec((rows * HALVES, part), lambda i: (0, 0)),
        out_shape=jax.ShapeDtypeStruct((rows * HALVES, part), BF16),
        scratch_shapes=[pltpu.VMEM((HALVES, rows, part), BF16)],
        compiler_params=pltpu.CompilerParams(vmem_limit_bytes=VMEM_BYTES),
    )(*acts, *weights)


def project_kernel(rows_ref, weight_ref, out_ref, turned):
    @pl.when(pl.program_id(0) == 0)
    def _():
        turned[...] = weight_ref[...].T

    columns = jnp.dot(rows_ref[...], turned[...], preferred_element_type=F32)
    out_ref[...] = columns.reshape(out_ref.shape).astype(BF16)


def project(rows, weight, owners):
    steps = 4
    group = rows.shape[0] // owners
    return pl.pallas_call(
        project_kernel,
        grid=(steps,),
        in_specs=[
            pl.BlockSpec((rows.shape[0] // steps, rows.shape[1]), lambda i: (i, 0)),
            pl.BlockSpec(weight.shape, lambda i: (0, 0)),
        ],
        out_specs=pl.BlockSpec((owners // steps, group, weight.shape[0]), lambda i: (i, 0, 0)),
        out_shape=jax.ShapeDtypeStruct((owners, group, weight.shape[0]), BF16),
        scratch_shapes=[pltpu.VMEM(weight.shape[::-1], BF16)],
        compiler_params=pltpu.CompilerParams(vmem_limit_bytes=VMEM_BYTES),
    )(rows, weight)


def settle_kernel(place_ref, x_ref, *refs):
    outs, wide = refs[:-1], refs[-1]
    quarters = len(outs)
    blocks, _, columns = x_ref.shape
    value = x_ref[...].astype(F32)
    per = blocks // quarters
    for block in range(blocks):
        at = (block % per) * columns
        wide[block // per, :, at : at + columns] = value[block]
    for k in range(quarters):
        outs[k][...] = wide[lax.rem(place_ref[0] + k, quarters)].astype(BF16)


def settle(place, x, quarters):
    blocks, rows, columns = x.shape
    width = blocks // quarters * columns
    return pl.pallas_call(
        settle_kernel,
        in_specs=[
            pl.BlockSpec(memory_space=pltpu.SMEM),
            pl.BlockSpec(memory_space=pltpu.VMEM),
        ],
        out_shape=[jax.ShapeDtypeStruct((rows, width), BF16) for _ in range(quarters)],
        scratch_shapes=[pltpu.VMEM((quarters, rows, width), F32)],
        compiler_params=pltpu.CompilerParams(vmem_limit_bytes=VMEM_BYTES),
    )(place, x)


def attend_kernel(scale, length_ref, q_ref, cache_ref, out_ref, highest, summed, total):
    step = pl.program_id(0)
    rows, latent = out_ref.shape
    chunk = cache_ref.shape[1]
    keys = cache_ref[...]
    values = keys[:latent].T
    valid = step * chunk + iota((1, chunk), 1) < length_ref[0]
    block = min(rows, 256)

    @pl.when(step == 0)
    def _():
        highest[...] = jnp.full_like(highest, -1e30)
        summed[...] = jnp.zeros_like(summed)
        total[...] = jnp.zeros_like(total)

    for at in range(0, rows, block):
        span = slice(at, at + block)
        scores = jnp.dot(q_ref[span, :], keys, preferred_element_type=F32)
        scores = jnp.where(valid, scores, -1e30)
        before = highest[span, :]
        now = jnp.maximum(before, jnp.max(scores, axis=1, keepdims=True))
        weights = jnp.exp2((scores - now) * scale)
        fade = jnp.exp2((before - now) * scale)
        highest[span, :] = now
        summed[span, :] = summed[span, :] * fade + jnp.sum(weights, axis=1, keepdims=True)
        total[span, :] = total[span, :] * fade + jnp.dot(
            weights.astype(BF16), values, preferred_element_type=F32
        )

    @pl.when(step == pl.num_programs(0) - 1)
    def _():
        out_ref[...] = (total[...] / summed[...]).astype(BF16)


def attend_request(query_block, cache_block, length, value_up, score_scale):
    depths, nodes, heads_dev, width_qk = query_block.shape
    latent = value_up.shape[1]
    query_rows = query_block.reshape(-1, width_qk)
    rows = query_rows.shape[0]
    chunk = 2048
    latent_out = pl.pallas_call(
        functools.partial(attend_kernel, score_scale * math.log2(math.e)),
        grid=(cache_block.shape[0] // chunk,),
        in_specs=[
            pl.BlockSpec(memory_space=pltpu.SMEM),
            pl.BlockSpec((rows, width_qk), lambda i: (0, 0)),
            pl.BlockSpec((width_qk, chunk), lambda i: (0, i)),
        ],
        out_specs=pl.BlockSpec((rows, latent), lambda i: (0, 0)),
        out_shape=jax.ShapeDtypeStruct((rows, latent), BF16),
        scratch_shapes=[
            pltpu.VMEM((rows, 1), F32),
            pltpu.VMEM((rows, 1), F32),
            pltpu.VMEM((rows, latent), F32),
        ],
        compiler_params=pltpu.CompilerParams(vmem_limit_bytes=VMEM_BYTES),
    )(length, query_rows, cache_block.T)
    latent_out = latent_out.reshape(depths * nodes, heads_dev, latent)
    mixed = jnp.einsum("nhl,hld->nhd", latent_out, value_up, preferred_element_type=F32)
    return mixed.astype(BF16).reshape(depths, nodes, -1)


def local(
    node_embed,
    embed_gain,
    root_hidden,
    parents,
    queries,
    cache,
    cache_len,
    value_up,
    out_proj,
    moe_gain,
    router,
    expert_ids,
    w_gate,
    w_up,
    w_down,
):
    depths, _, nodes, quarter = node_embed.shape
    groups = lax.axis_size("dp")
    tp = lax.axis_size("tp")
    mine = lax.axis_index("tp")
    width = quarter * tp
    part = quarter // HALVES
    experts = router.shape[1]
    latent = value_up.shape[1]
    score_scale = (value_up.shape[2] + cache.shape[2] - latent) ** (-0.5)
    shifts = {k: [(i, (i + k) % tp) for i in range(tp)] for k in range(1, tp)}

    def share(value):
        return [value] + [lax.ppermute(value, "tp", shifts[k]) for k in range(1, tp)]

    def deal(values):
        return [values[0]] + [lax.ppermute(values[k], "tp", shifts[k]) for k in range(1, tp)]

    heads = attend_request(queries[:, 0], cache[0], cache_len, value_up, score_scale)
    heads = heads.reshape(depths * nodes, -1)
    gathered = lax.all_gather(heads, "dp", axis=0, tiled=True)

    w_down, node_embed, heads = lax.optimization_barrier((w_down, node_embed, heads))
    down = deal(
        [
            lax.dynamic_slice(
                w_down[0], (0, (mine + k) % tp * quarter), (w_down.shape[1], quarter)
            )
            for k in range(tp)
        ]
    )
    embed = node_embed[:, 0].astype(F32)
    squares = jnp.sum(embed * embed, axis=-1).reshape(1, depths * nodes)
    gain_rows = quarter // 128
    notes = jnp.concatenate(
        [
            moe_gain.reshape(gain_rows, 128),
            jnp.pad(squares, ((0, 1), (0, 128 - depths * nodes))),
        ]
    )
    notes = jnp.stack(share(notes))
    embed_sq = jnp.sum(notes[:, gain_rows, : depths * nodes], axis=0).reshape(depths, nodes)
    normed = embed * (1.0 / jnp.sqrt(embed_sq / width + EPS))[..., None] * embed_gain
    gains = notes[(mine - jnp.arange(tp, dtype=jnp.int32)) % tp, :gain_rows].reshape(tp, HALVES, part)
    gathered, normed, gains, *down = lax.optimization_barrier((gathered, normed, gains, *down))
    columns = project(gathered, out_proj.T, groups)
    columns = lax.all_to_all(columns, "dp", split_axis=0, concat_axis=0, tiled=True)
    attn = deal(settle(mine.reshape(1).astype(jnp.int32), columns, tp))

    names = jnp.pad(parents[:, 0, :, None], ((1, 0), (0, 0), (0, 0)))
    tables = jnp.concatenate([expert_ids[:, 0], names], axis=2)
    drafted = []
    carried = None
    for depth in range(depths + 1):
        args = [tables]
        if depth == 0:
            args += [root_hidden, normed, *attn, router.T, moe_gain[None]]
        else:
            args += carried
        if 0 < depth < depths:
            args += [routed, base]
        result = list(owner_call(depth, depths, experts, width, tp, args, nodes, quarter))
        if depth > 0:
            drafted.append(result.pop(0))
        if depth == depths:
            break
        if depth == 0:
            routed, base = result.pop(-2), result.pop()
        state, stats, outgoing = result
        all_stats = share(stats)
        outgoing = outgoing.reshape(experts * tp, HALVES * SLOTS, part)
        arrived = lax.all_to_all(outgoing, ("dp", "tp"), split_axis=0, concat_axis=0, tiled=True)
        arrived = arrived.reshape(groups, tp, HALVES * SLOTS, part)
        act = expert_call(width, arrived, gains, w_gate[0], w_up[0])
        answer = down_call(share(act), down)
        answer = answer.reshape(groups, HALVES * SLOTS, part)
        returned = lax.all_to_all(answer, "dp", split_axis=0, concat_axis=0, tiled=True)
        carried = [returned.reshape(groups * HALVES * SLOTS, part), state] + all_stats
    return jnp.stack(drafted)[:, None]


def solution(mesh):
    placed = (
        P(None, "dp", None, "tp"),
        P("tp"),
        P("dp", "tp"),
        P(None, "dp", None),
        P(None, "dp", None, "tp", None),
        P("dp", None, None),
        P("dp"),
        P("tp", None, None),
        P("tp", "dp"),
        P("tp"),
        P("tp", None),
        P(None, "dp", None, None),
        P("dp", None, "tp"),
        P("dp", None, "tp"),
        P("dp", "tp", None),
    )
    return jax.shard_map(
        local, mesh=mesh, in_specs=placed, out_specs=P(None, "dp", None, "tp"), check_vma=False
    )
```

```python
import functools
import math

import jax
import jax.numpy as jnp
from jax import lax
from jax.experimental import pallas as pl
from jax.experimental.pallas import tpu as pltpu
from jax.sharding import PartitionSpec as P

EPS = 1e-06
ROUTE_SCALE = 2.5
SLOTS = 4
HALVES = 2
F32 = jnp.float32
BF16 = jnp.bfloat16
VMEM_BYTES = 48 * 1024 * 1024


def iota(shape, dim):
    return lax.broadcasted_iota(jnp.int32, shape, dim)


def split3(value):
    high = value.astype(BF16)
    rest = value - high.astype(F32)
    middle = rest.astype(BF16)
    low = (rest - middle.astype(F32)).astype(BF16)
    return high, middle, low


def pack_matrix(rows, forward):
    shape = (rows, rows)
    packed, mixed = iota(shape, 0 if forward else 1), iota(shape, 1 if forward else 0)
    per_half = rows // HALVES
    half = packed // per_half
    place = packed - half * per_half
    request = place // SLOTS
    source = request * (HALVES * SLOTS) + half * SLOTS + (place - request * SLOTS)
    return (source == mixed).astype(BF16)


def routing(ids, experts):
    nodes, top = ids.shape
    lane = iota((nodes, experts), 1)
    named = jnp.zeros((nodes, experts), F32)
    for route in range(top):
        named = named + (ids[:, route : route + 1] == lane).astype(F32)
    above = (iota((nodes, nodes), 1) < iota((nodes, nodes), 0)).astype(BF16)
    rank = jnp.dot(above, named.astype(BF16), preferred_element_type=F32)
    columns = experts * HALVES * SLOTS
    spread = (iota((experts, columns), 1) // (HALVES * SLOTS) == iota((experts, columns), 0)).astype(BF16)
    order = jnp.dot(((rank + 1.0) * named).astype(BF16), spread, preferred_element_type=F32)
    column = iota((nodes, columns), 1)
    slot = column - (column // SLOTS) * SLOTS
    placed = order == (slot + 1).astype(F32)
    half = (column // SLOTS) - (column // (HALVES * SLOTS)) * HALVES
    return named, spread, placed, half


def combine(rec, state, stats, ids, experts, width):
    nodes = ids.shape[0]
    named, spread, placed, half = routing(ids, experts)
    logits = stats[:, :experts]
    inv_rms = 1.0 / jnp.sqrt(stats[:, experts : experts + 1] / width + EPS)
    chosen = named / (1.0 + jnp.exp(-(logits * inv_rms)))
    weight = chosen / jnp.sum(chosen, axis=1, keepdims=True) * ROUTE_SCALE
    wide = jnp.dot(
        jnp.concatenate(split3(weight), axis=0), spread, preferred_element_type=F32
    )
    zero = jnp.zeros_like(placed, dtype=F32)
    pieces = []
    for h in range(HALVES):
        for piece in range(3):
            part = wide[piece * nodes : (piece + 1) * nodes]
            pieces.append(jnp.where(placed & (half == h), part, zero))
    mixing = jnp.concatenate(pieces, axis=0).astype(BF16)
    mixed = jnp.dot(mixing, rec, preferred_element_type=F32)
    outs = []
    for h in range(HALVES):
        base = h * 3 * nodes
        outs.append(
            mixed[base : base + nodes]
            + mixed[base + nodes : base + 2 * nodes]
            + mixed[base + 2 * nodes : base + 3 * nodes]
        )
    moe_out = jnp.concatenate(outs, axis=1)
    return (state.astype(F32) + moe_out).astype(BF16)


def owner_kernel(depth, depths, experts, width, copies, *refs):
    first, last = depth == 0, depth == depths
    refs = list(refs)
    tables = refs.pop(0)
    top = tables.shape[2] - 1
    if first:
        root = refs.pop(0)[...]
        start = refs.pop(0)[...]
        attn = refs.pop(0)[...].astype(F32)
        for _ in range(3):
            attn = attn + refs.pop(0)[...].astype(F32)
        start = start + attn.astype(BF16).astype(F32).reshape(start.shape)
        base, start = start[1:], start[0]
        router = refs.pop(0)[...].astype(F32)
        product = split3(router * refs.pop(0)[...])
        blank = jnp.zeros((128 - 3 * experts, router.shape[1]), BF16)
        routed = jnp.concatenate([*product, blank], axis=0)
    else:
        rec = refs.pop(0)[...]
        state_ref = refs.pop(0)
        stats = refs.pop(0)[...]
        for _ in range(3):
            stats = stats + refs.pop(0)[...]
    if not first and not last:
        routed = refs.pop(0)[...]
        start = refs.pop(0)[depth - 1]
    if not first:
        drafted_ref = refs.pop(0)
        drafted = combine(rec, state_ref[...], stats, tables[depth - 1][:, :top], experts, width)
        drafted_ref[...] = drafted
    if last:
        return
    out_state, out_stats, outgoing = refs[:3]
    if first:
        refs[3][...] = routed
        refs[4][...] = base
        previous = root.astype(F32)
    else:
        parents = tables[depth][:, top : top + 1]
        wide = drafted.astype(F32)
        previous = jnp.zeros_like(wide)
        for node in range(wide.shape[0]):
            previous = previous + jnp.where(parents == node, wide[node : node + 1, :], 0.0)
    state = (start + previous).astype(BF16)
    out_state[...] = state
    wide = state.astype(F32)
    square = jnp.sum(wide * wide, axis=1, keepdims=True)
    parts = lax.dot_general(
        state, routed, (((1,), (1,)), ((), ())), preferred_element_type=F32
    )
    logits = parts[:, :experts] + parts[:, experts : 2 * experts] + parts[:, 2 * experts : 3 * experts]
    pad = jnp.zeros((wide.shape[0], 128 - experts - 1), F32)
    out_stats[...] = jnp.concatenate([logits, square, pad], axis=1)
    _, _, placed, half = routing(tables[depth][:, :top], experts)
    table = jnp.concatenate(
        [(placed & (half == h)).astype(F32) for h in range(HALVES)], axis=0
    ).astype(BF16)
    part = wide.shape[1] // HALVES
    halves = jnp.concatenate(
        [wide[:, h * part : (h + 1) * part] for h in range(HALVES)], axis=0
    ).astype(BF16)
    sent = lax.dot_general(table, halves, (((0,), (0,)), ((), ())), preferred_element_type=F32)
    sent = sent.reshape(experts, HALVES * SLOTS, part).astype(BF16)
    for copy in range(copies):
        outgoing[:, copy] = sent


def owner_call(depth, depths, experts, width, copies, args, nodes, quarter):
    outs = []
    if depth > 0:
        outs.append(jax.ShapeDtypeStruct((nodes, quarter), BF16))
    if depth < depths:
        outs.append(jax.ShapeDtypeStruct((nodes, quarter), BF16))
        outs.append(jax.ShapeDtypeStruct((nodes, 128), F32))
        outs.append(
            jax.ShapeDtypeStruct((experts, copies, HALVES * SLOTS, quarter // HALVES), BF16)
        )
    if depth == 0:
        outs.append(jax.ShapeDtypeStruct((128, quarter), BF16))
        outs.append(jax.ShapeDtypeStruct((depths - 1, nodes, quarter), F32))
    return pl.pallas_call(
        functools.partial(owner_kernel, depth, depths, experts, width, copies),
        out_shape=outs,
        compiler_params=pltpu.CompilerParams(vmem_limit_bytes=VMEM_BYTES),
    )(*args)


def expert_kernel(width, x_ref, gain_ref, gate_ref, up_ref, act_ref, pack, square, total):
    step = pl.program_id(0)
    sources, _, group, part = x_ref.shape
    rows = sources * group
    per_half = rows // HALVES
    hidden = gate_ref.shape[1]

    @pl.when(step == 0)
    def _():
        pack[...] = pack_matrix(rows, True)
        square[...] = jnp.zeros_like(square)
        total[...] = jnp.zeros_like(total)

    mixed = x_ref[:, step].astype(F32).reshape(rows, part).astype(BF16)
    packed = jnp.dot(pack[...], mixed, preferred_element_type=F32)
    gain = gain_ref[step]
    for h in range(HALVES):
        piece = packed[h * per_half : (h + 1) * per_half]
        square[...] += jnp.sum(piece * piece, axis=1, keepdims=True)
        piece = (piece * gain[h : h + 1, :]).astype(BF16)
        span = slice(h * part, (h + 1) * part)
        total[:, :hidden] += jnp.dot(piece, gate_ref[span, :], preferred_element_type=F32)
        total[:, hidden:] += jnp.dot(piece, up_ref[span, :], preferred_element_type=F32)

    @pl.when(step == pl.num_programs(0) - 1)
    def _():
        inv = 1.0 / jnp.sqrt(square[...] / width + EPS)
        gate = total[:, :hidden] * inv
        act_ref[...] = (gate / (1.0 + jnp.exp(-gate)) * (total[:, hidden:] * inv)).astype(BF16)


def expert_call(width, x, gain, gate, up):
    sources, quarters, group, part = x.shape
    rows = sources * group
    hidden = gate.shape[1]
    block = gate.shape[0] // quarters
    return pl.pallas_call(
        functools.partial(expert_kernel, width),
        grid=(quarters,),
        in_specs=[
            pl.BlockSpec(x.shape, lambda i: (0, 0, 0, 0)),
            pl.BlockSpec(gain.shape, lambda i: (0, 0, 0)),
            pl.BlockSpec((block, hidden), lambda i: (i, 0)),
            pl.BlockSpec((block, hidden), lambda i: (i, 0)),
        ],
        out_specs=pl.BlockSpec((rows // HALVES, hidden), lambda i: (0, 0)),
        out_shape=jax.ShapeDtypeStruct((rows // HALVES, hidden), BF16),
        scratch_shapes=[
            pltpu.VMEM((rows, rows), BF16),
            pltpu.VMEM((rows // HALVES, 1), F32),
            pltpu.VMEM((rows // HALVES, 2 * hidden), F32),
        ],
        compiler_params=pltpu.CompilerParams(vmem_limit_bytes=VMEM_BYTES),
    )(x, gain, gate, up)


def down_kernel(count, *refs):
    acts, weights, out_ref, stacked = refs[:count], refs[count : 2 * count], *refs[2 * count :]
    step = pl.program_id(0)
    total = jnp.dot(acts[0][...], weights[0][...], preferred_element_type=F32)
    for index in range(1, count):
        total = total + jnp.dot(acts[index][...], weights[index][...], preferred_element_type=F32)
    stacked[step] = total.astype(BF16)

    @pl.when(step == HALVES - 1)
    def _():
        rows, part = out_ref.shape
        unpack = pack_matrix(rows, False)
        value = stacked[...].reshape(rows, part)
        out_ref[...] = jnp.dot(unpack, value, preferred_element_type=F32).astype(BF16)


def down_call(acts, weights):
    rows = acts[0].shape[0]
    hidden, quarter = weights[0].shape
    part = quarter // HALVES
    return pl.pallas_call(
        functools.partial(down_kernel, len(acts)),
        grid=(HALVES,),
        in_specs=[pl.BlockSpec(acts[0].shape, lambda i: (0, 0)) for _ in acts]
        + [pl.BlockSpec((hidden, part), lambda i: (0, i)) for _ in weights],
        out_specs=pl.BlockSpec((rows * HALVES, part), lambda i: (0, 0)),
        out_shape=jax.ShapeDtypeStruct((rows * HALVES, part), BF16),
        scratch_shapes=[pltpu.VMEM((HALVES, rows, part), BF16)],
        compiler_params=pltpu.CompilerParams(vmem_limit_bytes=VMEM_BYTES),
    )(*acts, *weights)


def turn_kernel(weight_ref, out_ref):
    out_ref[...] = weight_ref[...].T


def turn(weight):
    return pl.pallas_call(
        turn_kernel,
        out_shape=jax.ShapeDtypeStruct(weight.shape[::-1], weight.dtype),
        compiler_params=pltpu.CompilerParams(vmem_limit_bytes=VMEM_BYTES),
    )(weight)


def project_kernel(rows_ref, weight_ref, out_ref):
    columns = jnp.dot(rows_ref[...], weight_ref[...], preferred_element_type=F32)
    out_ref[...] = columns.reshape(out_ref.shape).astype(BF16)


def project(rows, weight, owners):
    steps = 4
    group = rows.shape[0] // owners
    return pl.pallas_call(
        project_kernel,
        grid=(steps,),
        in_specs=[
            pl.BlockSpec((rows.shape[0] // steps, rows.shape[1]), lambda i: (i, 0)),
            pl.BlockSpec(weight.shape, lambda i: (0, 0)),
        ],
        out_specs=pl.BlockSpec((owners // steps, group, weight.shape[1]), lambda i: (i, 0, 0)),
        out_shape=jax.ShapeDtypeStruct((owners, group, weight.shape[1]), BF16),
        compiler_params=pltpu.CompilerParams(vmem_limit_bytes=VMEM_BYTES),
    )(rows, weight)


def settle_kernel(place_ref, x_ref, *refs):
    outs, wide = refs[:-1], refs[-1]
    quarters = len(outs)
    blocks, _, columns = x_ref.shape
    value = x_ref[...].astype(F32)
    per = blocks // quarters
    for block in range(blocks):
        at = (block % per) * columns
        wide[block // per, :, at : at + columns] = value[block]
    for k in range(quarters):
        outs[k][...] = wide[lax.rem(place_ref[0] + k, quarters)].astype(BF16)


def settle(place, x, quarters):
    blocks, rows, columns = x.shape
    width = blocks // quarters * columns
    return pl.pallas_call(
        settle_kernel,
        in_specs=[
            pl.BlockSpec(memory_space=pltpu.SMEM),
            pl.BlockSpec(memory_space=pltpu.VMEM),
        ],
        out_shape=[jax.ShapeDtypeStruct((rows, width), BF16) for _ in range(quarters)],
        scratch_shapes=[pltpu.VMEM((quarters, rows, width), F32)],
        compiler_params=pltpu.CompilerParams(vmem_limit_bytes=VMEM_BYTES),
    )(place, x)


def attend_kernel(scale, length_ref, q_ref, cache_ref, out_ref, highest, summed, total):
    step = pl.program_id(0)
    rows, latent = out_ref.shape
    chunk = cache_ref.shape[1]
    keys = cache_ref[...]
    values = keys[:latent].T
    valid = step * chunk + iota((1, chunk), 1) < length_ref[0]
    block = min(rows, 256)

    @pl.when(step == 0)
    def _():
        highest[...] = jnp.full_like(highest, -1e30)
        summed[...] = jnp.zeros_like(summed)
        total[...] = jnp.zeros_like(total)

    def score(at):
        return jnp.dot(q_ref[at : at + block, :], keys, preferred_element_type=F32)

    ahead = score(0)
    for at in range(0, rows, block):
        span = slice(at, at + block)
        scores = jnp.where(valid, ahead, -1e30)
        if at + block < rows:
            ahead = score(at + block)
        before = highest[span, :]
        now = jnp.maximum(before, jnp.max(scores, axis=1, keepdims=True))
        weights = jnp.exp2((scores - now) * scale)
        fade = jnp.exp2((before - now) * scale)
        highest[span, :] = now
        summed[span, :] = summed[span, :] * fade + jnp.sum(weights, axis=1, keepdims=True)
        total[span, :] = total[span, :] * fade + jnp.dot(
            weights.astype(BF16), values, preferred_element_type=F32
        )

    @pl.when(step == pl.num_programs(0) - 1)
    def _():
        out_ref[...] = (total[...] / summed[...]).astype(BF16)


def attend_request(query_block, cache_block, length, value_up, score_scale):
    depths, nodes, heads_dev, width_qk = query_block.shape
    latent = value_up.shape[1]
    query_rows = query_block.reshape(-1, width_qk)
    rows = query_rows.shape[0]
    chunk = 1024
    latent_out = pl.pallas_call(
        functools.partial(attend_kernel, score_scale * math.log2(math.e)),
        grid=(cache_block.shape[0] // chunk,),
        in_specs=[
            pl.BlockSpec(memory_space=pltpu.SMEM),
            pl.BlockSpec((rows, width_qk), lambda i: (0, 0)),
            pl.BlockSpec((width_qk, chunk), lambda i: (0, i)),
        ],
        out_specs=pl.BlockSpec((rows, latent), lambda i: (0, 0)),
        out_shape=jax.ShapeDtypeStruct((rows, latent), BF16),
        scratch_shapes=[
            pltpu.VMEM((rows, 1), F32),
            pltpu.VMEM((rows, 1), F32),
            pltpu.VMEM((rows, latent), F32),
        ],
        compiler_params=pltpu.CompilerParams(vmem_limit_bytes=VMEM_BYTES),
    )(length, query_rows, cache_block.T)
    latent_out = latent_out.reshape(depths * nodes, heads_dev, latent)
    mixed = jnp.einsum("nhl,hld->nhd", latent_out, value_up, preferred_element_type=F32)
    return mixed.astype(BF16).reshape(depths, nodes, -1)


def local(
    node_embed,
    embed_gain,
    root_hidden,
    parents,
    queries,
    cache,
    cache_len,
    value_up,
    out_proj,
    moe_gain,
    router,
    expert_ids,
    w_gate,
    w_up,
    w_down,
):
    depths, _, nodes, quarter = node_embed.shape
    groups = lax.axis_size("dp")
    tp = lax.axis_size("tp")
    mine = lax.axis_index("tp")
    width = quarter * tp
    part = quarter // HALVES
    experts = router.shape[1]
    latent = value_up.shape[1]
    score_scale = (value_up.shape[2] + cache.shape[2] - latent) ** (-0.5)
    shifts = {k: [(i, (i + k) % tp) for i in range(tp)] for k in range(1, tp)}

    def share(value):
        return [value] + [lax.ppermute(value, "tp", shifts[k]) for k in range(1, tp)]

    def deal(values):
        return [values[0]] + [lax.ppermute(values[k], "tp", shifts[k]) for k in range(1, tp)]

    heads = attend_request(queries[:, 0], cache[0], cache_len, value_up, score_scale)
    heads = heads.reshape(depths * nodes, -1)
    gathered = lax.all_gather(heads, "dp", axis=0, tiled=True)

    w_down, node_embed, heads = lax.optimization_barrier((w_down, node_embed, heads))
    down = deal(
        [
            lax.dynamic_slice(
                w_down[0], (0, (mine + k) % tp * quarter), (w_down.shape[1], quarter)
            )
            for k in range(tp)
        ]
    )
    embed = node_embed[:, 0].astype(F32)
    squares = jnp.sum(embed * embed, axis=-1).reshape(1, depths * nodes)
    gain_rows = quarter // 128
    notes = jnp.concatenate(
        [
            moe_gain.reshape(gain_rows, 128),
            jnp.pad(squares, ((0, 1), (0, 128 - depths * nodes))),
        ]
    )
    notes = jnp.stack(share(notes))
    embed_sq = jnp.sum(notes[:, gain_rows, : depths * nodes], axis=0).reshape(depths, nodes)
    normed = embed * (1.0 / jnp.sqrt(embed_sq / width + EPS))[..., None] * embed_gain
    gains = notes[(mine - jnp.arange(tp, dtype=jnp.int32)) % tp, :gain_rows].reshape(tp, HALVES, part)
    turned, heads = lax.optimization_barrier((out_proj.T, heads))
    turned = turn(turned)
    gathered, normed, gains, turned, *down = lax.optimization_barrier(
        (gathered, normed, gains, turned, *down)
    )
    columns = project(gathered, turned, groups)
    columns = lax.all_to_all(columns, "dp", split_axis=0, concat_axis=0, tiled=True)
    attn = deal(settle(mine.reshape(1).astype(jnp.int32), columns, tp))

    names = jnp.pad(parents[:, 0, :, None], ((1, 0), (0, 0), (0, 0)))
    tables = jnp.concatenate([expert_ids[:, 0], names], axis=2)
    drafted = []
    carried = None
    for depth in range(depths + 1):
        args = [tables]
        if depth == 0:
            args += [root_hidden, normed, *attn, router.T, moe_gain[None]]
        else:
            args += carried
        if 0 < depth < depths:
            args += [routed, base]
        result = list(owner_call(depth, depths, experts, width, tp, args, nodes, quarter))
        if depth > 0:
            drafted.append(result.pop(0))
        if depth == depths:
            break
        if depth == 0:
            routed, base = result.pop(-2), result.pop()
        state, stats, outgoing = result
        all_stats = share(stats)
        outgoing = outgoing.reshape(experts * tp, HALVES * SLOTS, part)
        arrived = lax.all_to_all(outgoing, ("dp", "tp"), split_axis=0, concat_axis=0, tiled=True)
        arrived = arrived.reshape(groups, tp, HALVES * SLOTS, part)
        act = expert_call(width, arrived, gains, w_gate[0], w_up[0])
        answer = down_call(share(act), down)
        answer = answer.reshape(groups, HALVES * SLOTS, part)
        returned = lax.all_to_all(answer, "dp", split_axis=0, concat_axis=0, tiled=True)
        carried = [returned.reshape(groups * HALVES * SLOTS, part), state] + all_stats
    return jnp.stack(drafted)[:, None]


def solution(mesh):
    placed = (
        P(None, "dp", None, "tp"),
        P("tp"),
        P("dp", "tp"),
        P(None, "dp", None),
        P(None, "dp", None, "tp", None),
        P("dp", None, None),
        P("dp"),
        P("tp", None, None),
        P("tp", "dp"),
        P("tp"),
        P("tp", None),
        P(None, "dp", None, None),
        P("dp", None, "tp"),
        P("dp", None, "tp"),
        P("dp", "tp", None),
    )
    return jax.shard_map(
        local, mesh=mesh, in_specs=placed, out_specs=P(None, "dp", None, "tp"), check_vma=False
    )
```

```python
import functools
import math

import jax
import jax.numpy as jnp
from jax import lax
from jax.experimental import pallas as pl
from jax.experimental.pallas import tpu as pltpu
from jax.sharding import PartitionSpec as P

EPS = 1e-06
ROUTE_SCALE = 2.5
SLOTS = 4
HALVES = 2
F32 = jnp.float32
BF16 = jnp.bfloat16
VMEM_BYTES = 48 * 1024 * 1024


def iota(shape, dim):
    return lax.broadcasted_iota(jnp.int32, shape, dim)


def split3(value):
    high = value.astype(BF16)
    rest = value - high.astype(F32)
    middle = rest.astype(BF16)
    low = (rest - middle.astype(F32)).astype(BF16)
    return high, middle, low


def pack_matrix(rows, forward):
    shape = (rows, rows)
    packed, mixed = iota(shape, 0 if forward else 1), iota(shape, 1 if forward else 0)
    per_half = rows // HALVES
    half = packed // per_half
    place = packed - half * per_half
    request = place // SLOTS
    source = request * (HALVES * SLOTS) + half * SLOTS + (place - request * SLOTS)
    return (source == mixed).astype(BF16)


def routing(ids, experts):
    nodes, top = ids.shape
    lane = iota((nodes, experts), 1)
    named = jnp.zeros((nodes, experts), F32)
    for route in range(top):
        named = named + (ids[:, route : route + 1] == lane).astype(F32)
    above = (iota((nodes, nodes), 1) < iota((nodes, nodes), 0)).astype(BF16)
    rank = jnp.dot(above, named.astype(BF16), preferred_element_type=F32)
    columns = experts * HALVES * SLOTS
    spread = (iota((experts, columns), 1) // (HALVES * SLOTS) == iota((experts, columns), 0)).astype(BF16)
    order = jnp.dot(((rank + 1.0) * named).astype(BF16), spread, preferred_element_type=F32)
    column = iota((nodes, columns), 1)
    slot = column - (column // SLOTS) * SLOTS
    placed = order == (slot + 1).astype(F32)
    half = (column // SLOTS) - (column // (HALVES * SLOTS)) * HALVES
    return named, spread, placed, half


def combine(rec, state, stats, ids, experts, width):
    nodes = ids.shape[0]
    named, spread, placed, half = routing(ids, experts)
    logits = stats[:, :experts]
    inv_rms = 1.0 / jnp.sqrt(stats[:, experts : experts + 1] / width + EPS)
    chosen = named / (1.0 + jnp.exp(-(logits * inv_rms)))
    weight = chosen / jnp.sum(chosen, axis=1, keepdims=True) * ROUTE_SCALE
    wide = jnp.dot(
        jnp.concatenate(split3(weight), axis=0), spread, preferred_element_type=F32
    )
    zero = jnp.zeros_like(placed, dtype=F32)
    pieces = []
    for h in range(HALVES):
        for piece in range(3):
            part = wide[piece * nodes : (piece + 1) * nodes]
            pieces.append(jnp.where(placed & (half == h), part, zero))
    mixing = jnp.concatenate(pieces, axis=0).astype(BF16)
    mixed = jnp.dot(mixing, rec, preferred_element_type=F32)
    outs = []
    for h in range(HALVES):
        base = h * 3 * nodes
        outs.append(
            mixed[base : base + nodes]
            + mixed[base + nodes : base + 2 * nodes]
            + mixed[base + 2 * nodes : base + 3 * nodes]
        )
    moe_out = jnp.concatenate(outs, axis=1)
    return (state.astype(F32) + moe_out).astype(BF16)


def owner_kernel(depth, depths, experts, width, copies, *refs):
    first, last = depth == 0, depth == depths
    refs = list(refs)
    tables = refs.pop(0)
    top = tables.shape[2] - 1
    if first:
        root = refs.pop(0)[...]
        start = refs.pop(0)[...]
        attn = refs.pop(0)[...].astype(F32)
        for _ in range(3):
            attn = attn + refs.pop(0)[...].astype(F32)
        start = start + attn.astype(BF16).astype(F32).reshape(start.shape)
        base, start = start[1:], start[0]
        router = refs.pop(0)[...].astype(F32)
        product = split3(router * refs.pop(0)[...])
        blank = jnp.zeros((128 - 3 * experts, router.shape[1]), BF16)
        routed = jnp.concatenate([*product, blank], axis=0)
    else:
        rec = refs.pop(0)[...]
        state_ref = refs.pop(0)
        stats = refs.pop(0)[...]
        for _ in range(3):
            stats = stats + refs.pop(0)[...]
    if not first and not last:
        routed = refs.pop(0)[...]
        start = refs.pop(0)[depth - 1]
    if not first:
        drafted_ref = refs.pop(0)
        drafted = combine(rec, state_ref[...], stats, tables[depth - 1][:, :top], experts, width)
        drafted_ref[...] = drafted
    if last:
        return
    out_state, out_stats, outgoing = refs[:3]
    if first:
        refs[3][...] = routed
        refs[4][...] = base
        previous = root.astype(F32)
    else:
        parents = tables[depth][:, top : top + 1]
        wide = drafted.astype(F32)
        previous = jnp.zeros_like(wide)
        for node in range(wide.shape[0]):
            previous = previous + jnp.where(parents == node, wide[node : node + 1, :], 0.0)
    state = (start + previous).astype(BF16)
    out_state[...] = state
    wide = state.astype(F32)
    square = jnp.sum(wide * wide, axis=1, keepdims=True)
    parts = lax.dot_general(
        state, routed, (((1,), (1,)), ((), ())), preferred_element_type=F32
    )
    logits = parts[:, :experts] + parts[:, experts : 2 * experts] + parts[:, 2 * experts : 3 * experts]
    pad = jnp.zeros((wide.shape[0], 128 - experts - 1), F32)
    out_stats[...] = jnp.concatenate([logits, square, pad], axis=1)
    _, _, placed, half = routing(tables[depth][:, :top], experts)
    table = jnp.concatenate(
        [(placed & (half == h)).astype(F32) for h in range(HALVES)], axis=0
    ).astype(BF16)
    part = wide.shape[1] // HALVES
    halves = jnp.concatenate(
        [wide[:, h * part : (h + 1) * part] for h in range(HALVES)], axis=0
    ).astype(BF16)
    sent = lax.dot_general(table, halves, (((0,), (0,)), ((), ())), preferred_element_type=F32)
    sent = sent.reshape(experts, HALVES * SLOTS, part).astype(BF16)
    for copy in range(copies):
        outgoing[:, copy] = sent


def owner_call(depth, depths, experts, width, copies, args, nodes, quarter):
    outs = []
    if depth > 0:
        outs.append(jax.ShapeDtypeStruct((nodes, quarter), BF16))
    if depth < depths:
        outs.append(jax.ShapeDtypeStruct((nodes, quarter), BF16))
        outs.append(jax.ShapeDtypeStruct((nodes, 128), F32))
        outs.append(
            jax.ShapeDtypeStruct((experts, copies, HALVES * SLOTS, quarter // HALVES), BF16)
        )
    if depth == 0:
        outs.append(jax.ShapeDtypeStruct((128, quarter), BF16))
        outs.append(jax.ShapeDtypeStruct((depths - 1, nodes, quarter), F32))
    return pl.pallas_call(
        functools.partial(owner_kernel, depth, depths, experts, width, copies),
        out_shape=outs,
        compiler_params=pltpu.CompilerParams(vmem_limit_bytes=VMEM_BYTES),
    )(*args)


def expert_kernel(width, x_ref, gain_ref, gate_ref, up_ref, act_ref, pack, square, total):
    step = pl.program_id(0)
    sources, quarters, group, part = x_ref.shape
    rows = sources * group
    per_half = rows // HALVES
    hidden = gate_ref.shape[1]

    @pl.when(step == 0)
    def _():
        pack[...] = pack_matrix(rows, True)
        square[...] = jnp.zeros_like(square)
        total[...] = jnp.zeros_like(total)

    each = quarters // 2
    for turn_index in range(each):
        at = step * each + turn_index
        mixed = x_ref[:, at].astype(F32).reshape(rows, part).astype(BF16)
        packed = jnp.dot(pack[...], mixed, preferred_element_type=F32)
        gain = gain_ref[at]
        for h in range(HALVES):
            piece = packed[h * per_half : (h + 1) * per_half]
            square[...] += jnp.sum(piece * piece, axis=1, keepdims=True)
            piece = (piece * gain[h : h + 1, :]).astype(BF16)
            start = (turn_index * HALVES + h) * part
            span = slice(start, start + part)
            total[:, :hidden] += jnp.dot(piece, gate_ref[span, :], preferred_element_type=F32)
            total[:, hidden:] += jnp.dot(piece, up_ref[span, :], preferred_element_type=F32)

    @pl.when(step == pl.num_programs(0) - 1)
    def _():
        inv = 1.0 / jnp.sqrt(square[...] / width + EPS)
        gate = total[:, :hidden] * inv
        act_ref[...] = (gate / (1.0 + jnp.exp(-gate)) * (total[:, hidden:] * inv)).astype(BF16)


def expert_call(width, x, gain, gate, up):
    sources, quarters, group, part = x.shape
    rows = sources * group
    hidden = gate.shape[1]
    block = gate.shape[0] // 2
    return pl.pallas_call(
        functools.partial(expert_kernel, width),
        grid=(2,),
        in_specs=[
            pl.BlockSpec(x.shape, lambda i: (0, 0, 0, 0)),
            pl.BlockSpec(gain.shape, lambda i: (0, 0, 0)),
            pl.BlockSpec((block, hidden), lambda i: (i, 0)),
            pl.BlockSpec((block, hidden), lambda i: (i, 0)),
        ],
        out_specs=pl.BlockSpec((rows // HALVES, hidden), lambda i: (0, 0)),
        out_shape=jax.ShapeDtypeStruct((rows // HALVES, hidden), BF16),
        scratch_shapes=[
            pltpu.VMEM((rows, rows), BF16),
            pltpu.VMEM((rows // HALVES, 1), F32),
            pltpu.VMEM((rows // HALVES, 2 * hidden), F32),
        ],
        compiler_params=pltpu.CompilerParams(vmem_limit_bytes=VMEM_BYTES),
    )(x, gain, gate, up)


def down_kernel(count, *refs):
    acts, weights, out_ref, stacked = refs[:count], refs[count : 2 * count], *refs[2 * count :]
    step = pl.program_id(0)
    total = jnp.dot(acts[0][...], weights[0][...], preferred_element_type=F32)
    for index in range(1, count):
        total = total + jnp.dot(acts[index][...], weights[index][...], preferred_element_type=F32)
    stacked[step] = total.astype(BF16)

    @pl.when(step == HALVES - 1)
    def _():
        rows, part = out_ref.shape
        unpack = pack_matrix(rows, False)
        value = stacked[...].reshape(rows, part)
        out_ref[...] = jnp.dot(unpack, value, preferred_element_type=F32).astype(BF16)


def down_call(acts, weights):
    rows = acts[0].shape[0]
    hidden, quarter = weights[0].shape
    part = quarter // HALVES
    return pl.pallas_call(
        functools.partial(down_kernel, len(acts)),
        grid=(HALVES,),
        in_specs=[pl.BlockSpec(acts[0].shape, lambda i: (0, 0)) for _ in acts]
        + [pl.BlockSpec((hidden, part), lambda i: (0, i)) for _ in weights],
        out_specs=pl.BlockSpec((rows * HALVES, part), lambda i: (0, 0)),
        out_shape=jax.ShapeDtypeStruct((rows * HALVES, part), BF16),
        scratch_shapes=[pltpu.VMEM((HALVES, rows, part), BF16)],
        compiler_params=pltpu.CompilerParams(vmem_limit_bytes=VMEM_BYTES),
    )(*acts, *weights)


def turn_kernel(weight_ref, out_ref):
    out_ref[...] = weight_ref[...].T


def turn(weight):
    return pl.pallas_call(
        turn_kernel,
        out_shape=jax.ShapeDtypeStruct(weight.shape[::-1], weight.dtype),
        compiler_params=pltpu.CompilerParams(vmem_limit_bytes=VMEM_BYTES),
    )(weight)


def project_kernel(rows_ref, weight_ref, out_ref):
    columns = jnp.dot(rows_ref[...], weight_ref[...], preferred_element_type=F32)
    out_ref[...] = columns.reshape(out_ref.shape).astype(BF16)


def project(rows, weight, owners):
    steps = 4
    group = rows.shape[0] // owners
    return pl.pallas_call(
        project_kernel,
        grid=(steps,),
        in_specs=[
            pl.BlockSpec((rows.shape[0] // steps, rows.shape[1]), lambda i: (i, 0)),
            pl.BlockSpec(weight.shape, lambda i: (0, 0)),
        ],
        out_specs=pl.BlockSpec((owners // steps, group, weight.shape[1]), lambda i: (i, 0, 0)),
        out_shape=jax.ShapeDtypeStruct((owners, group, weight.shape[1]), BF16),
        compiler_params=pltpu.CompilerParams(vmem_limit_bytes=VMEM_BYTES),
    )(rows, weight)


def settle_kernel(place_ref, x_ref, *refs):
    outs, wide = refs[:-1], refs[-1]
    quarters = len(outs)
    blocks, _, columns = x_ref.shape
    value = x_ref[...].astype(F32)
    per = blocks // quarters
    for block in range(blocks):
        at = (block % per) * columns
        wide[block // per, :, at : at + columns] = value[block]
    for k in range(quarters):
        outs[k][...] = wide[lax.rem(place_ref[0] + k, quarters)].astype(BF16)


def settle(place, x, quarters):
    blocks, rows, columns = x.shape
    width = blocks // quarters * columns
    return pl.pallas_call(
        settle_kernel,
        in_specs=[
            pl.BlockSpec(memory_space=pltpu.SMEM),
            pl.BlockSpec(memory_space=pltpu.VMEM),
        ],
        out_shape=[jax.ShapeDtypeStruct((rows, width), BF16) for _ in range(quarters)],
        scratch_shapes=[pltpu.VMEM((quarters, rows, width), F32)],
        compiler_params=pltpu.CompilerParams(vmem_limit_bytes=VMEM_BYTES),
    )(place, x)


def attend_kernel(scale, length_ref, q_ref, cache_ref, out_ref, highest, summed, total):
    step = pl.program_id(0)
    rows, latent = out_ref.shape
    chunk = cache_ref.shape[1]
    keys = cache_ref[...]
    values = keys[:latent].T
    valid = step * chunk + iota((1, chunk), 1) < length_ref[0]
    block = min(rows, 256)

    @pl.when(step == 0)
    def _():
        highest[...] = jnp.full_like(highest, -1e30)
        summed[...] = jnp.zeros_like(summed)
        total[...] = jnp.zeros_like(total)

    def score(at):
        return jnp.dot(q_ref[at : at + block, :], keys, preferred_element_type=F32)

    ahead = score(0)
    for at in range(0, rows, block):
        span = slice(at, at + block)
        scores = jnp.where(valid, ahead, -1e30)
        if at + block < rows:
            ahead = score(at + block)
        before = highest[span, :]
        now = jnp.maximum(before, jnp.max(scores, axis=1, keepdims=True))
        weights = jnp.exp2((scores - now) * scale)
        fade = jnp.exp2((before - now) * scale)
        highest[span, :] = now
        summed[span, :] = summed[span, :] * fade + jnp.sum(weights, axis=1, keepdims=True)
        total[span, :] = total[span, :] * fade + jnp.dot(
            weights.astype(BF16), values, preferred_element_type=F32
        )

    @pl.when(step == pl.num_programs(0) - 1)
    def _():
        out_ref[...] = (total[...] / summed[...]).astype(BF16)


def attend_request(query_block, cache_block, length, value_up, score_scale):
    depths, nodes, heads_dev, width_qk = query_block.shape
    latent = value_up.shape[1]
    query_rows = query_block.reshape(-1, width_qk)
    rows = query_rows.shape[0]
    chunk = 1024
    latent_out = pl.pallas_call(
        functools.partial(attend_kernel, score_scale * math.log2(math.e)),
        grid=(cache_block.shape[0] // chunk,),
        in_specs=[
            pl.BlockSpec(memory_space=pltpu.SMEM),
            pl.BlockSpec((rows, width_qk), lambda i: (0, 0)),
            pl.BlockSpec((width_qk, chunk), lambda i: (0, i)),
        ],
        out_specs=pl.BlockSpec((rows, latent), lambda i: (0, 0)),
        out_shape=jax.ShapeDtypeStruct((rows, latent), BF16),
        scratch_shapes=[
            pltpu.VMEM((rows, 1), F32),
            pltpu.VMEM((rows, 1), F32),
            pltpu.VMEM((rows, latent), F32),
        ],
        compiler_params=pltpu.CompilerParams(vmem_limit_bytes=VMEM_BYTES),
    )(length, query_rows, cache_block.T)
    latent_out = latent_out.reshape(depths * nodes, heads_dev, latent)
    mixed = jnp.einsum("nhl,hld->nhd", latent_out, value_up, preferred_element_type=F32)
    return mixed.astype(BF16).reshape(depths, nodes, -1)


def local(
    node_embed,
    embed_gain,
    root_hidden,
    parents,
    queries,
    cache,
    cache_len,
    value_up,
    out_proj,
    moe_gain,
    router,
    expert_ids,
    w_gate,
    w_up,
    w_down,
):
    depths, _, nodes, quarter = node_embed.shape
    groups = lax.axis_size("dp")
    tp = lax.axis_size("tp")
    mine = lax.axis_index("tp")
    width = quarter * tp
    part = quarter // HALVES
    experts = router.shape[1]
    latent = value_up.shape[1]
    score_scale = (value_up.shape[2] + cache.shape[2] - latent) ** (-0.5)
    shifts = {k: [(i, (i + k) % tp) for i in range(tp)] for k in range(1, tp)}

    def share(value):
        return [value] + [lax.ppermute(value, "tp", shifts[k]) for k in range(1, tp)]

    def deal(values):
        return [values[0]] + [lax.ppermute(values[k], "tp", shifts[k]) for k in range(1, tp)]

    heads = attend_request(queries[:, 0], cache[0], cache_len, value_up, score_scale)
    heads = heads.reshape(depths * nodes, -1)
    gathered = lax.all_gather(heads, "dp", axis=0, tiled=True)

    w_down, node_embed, heads = lax.optimization_barrier((w_down, node_embed, heads))
    down = deal(
        [
            lax.dynamic_slice(
                w_down[0], (0, (mine + k) % tp * quarter), (w_down.shape[1], quarter)
            )
            for k in range(tp)
        ]
    )
    embed = node_embed[:, 0].astype(F32)
    squares = jnp.sum(embed * embed, axis=-1).reshape(1, depths * nodes)
    gain_rows = quarter // 128
    notes = jnp.concatenate(
        [
            moe_gain.reshape(gain_rows, 128),
            jnp.pad(squares, ((0, 1), (0, 128 - depths * nodes))),
        ]
    )
    notes = jnp.stack(share(notes))
    embed_sq = jnp.sum(notes[:, gain_rows, : depths * nodes], axis=0).reshape(depths, nodes)
    normed = embed * (1.0 / jnp.sqrt(embed_sq / width + EPS))[..., None] * embed_gain
    gains = notes[(mine - jnp.arange(tp, dtype=jnp.int32)) % tp, :gain_rows].reshape(tp, HALVES, part)
    turned, heads = lax.optimization_barrier((out_proj.T, heads))
    turned = turn(turned)
    gathered, normed, gains, turned, *down = lax.optimization_barrier(
        (gathered, normed, gains, turned, *down)
    )
    columns = project(gathered, turned, groups)
    columns = lax.all_to_all(columns, "dp", split_axis=0, concat_axis=0, tiled=True)
    attn = deal(settle(mine.reshape(1).astype(jnp.int32), columns, tp))

    names = jnp.pad(parents[:, 0, :, None], ((1, 0), (0, 0), (0, 0)))
    tables = jnp.concatenate([expert_ids[:, 0], names], axis=2)
    drafted = []
    carried = None
    for depth in range(depths + 1):
        args = [tables]
        if depth == 0:
            args += [root_hidden, normed, *attn, router.T, moe_gain[None]]
        else:
            args += carried
        if 0 < depth < depths:
            args += [routed, base]
        result = list(owner_call(depth, depths, experts, width, tp, args, nodes, quarter))
        if depth > 0:
            drafted.append(result.pop(0))
        if depth == depths:
            break
        if depth == 0:
            routed, base = result.pop(-2), result.pop()
        state, stats, outgoing = result
        all_stats = share(stats)
        outgoing = outgoing.reshape(experts * tp, HALVES * SLOTS, part)
        arrived = lax.all_to_all(outgoing, ("dp", "tp"), split_axis=0, concat_axis=0, tiled=True)
        arrived = arrived.reshape(groups, tp, HALVES * SLOTS, part)
        act = expert_call(width, arrived, gains, w_gate[0], w_up[0])
        answer = down_call(share(act), down)
        answer = answer.reshape(groups, HALVES * SLOTS, part)
        returned = lax.all_to_all(answer, "dp", split_axis=0, concat_axis=0, tiled=True)
        carried = [returned.reshape(groups * HALVES * SLOTS, part), state] + all_stats
    return jnp.stack(drafted)[:, None]


def solution(mesh):
    placed = (
        P(None, "dp", None, "tp"),
        P("tp"),
        P("dp", "tp"),
        P(None, "dp", None),
        P(None, "dp", None, "tp", None),
        P("dp", None, None),
        P("dp"),
        P("tp", None, None),
        P("tp", "dp"),
        P("tp"),
        P("tp", None),
        P(None, "dp", None, None),
        P("dp", None, "tp"),
        P("dp", None, "tp"),
        P("dp", "tp", None),
    )
    return jax.shard_map(
        local, mesh=mesh, in_specs=placed, out_specs=P(None, "dp", None, "tp"), check_vma=False
    )
```

```python
import functools
import math

import jax
import jax.numpy as jnp
from jax import lax
from jax.experimental import pallas as pl
from jax.experimental.pallas import tpu as pltpu
from jax.sharding import PartitionSpec as P

EPS = 1e-06
ROUTE_SCALE = 2.5
SLOTS = 4
HALVES = 2
F32 = jnp.float32
BF16 = jnp.bfloat16
VMEM_BYTES = 48 * 1024 * 1024


def iota(shape, dim):
    return lax.broadcasted_iota(jnp.int32, shape, dim)


def split3(value):
    high = value.astype(BF16)
    rest = value - high.astype(F32)
    middle = rest.astype(BF16)
    low = (rest - middle.astype(F32)).astype(BF16)
    return high, middle, low


def pack_matrix(rows, forward):
    shape = (rows, rows)
    packed, mixed = iota(shape, 0 if forward else 1), iota(shape, 1 if forward else 0)
    per_half = rows // HALVES
    half = packed // per_half
    place = packed - half * per_half
    request = place // SLOTS
    source = request * (HALVES * SLOTS) + half * SLOTS + (place - request * SLOTS)
    return (source == mixed).astype(BF16)


def routing(ids, experts):
    nodes, top = ids.shape
    lane = iota((nodes, experts), 1)
    named = jnp.zeros((nodes, experts), F32)
    for route in range(top):
        named = named + (ids[:, route : route + 1] == lane).astype(F32)
    above = (iota((nodes, nodes), 1) < iota((nodes, nodes), 0)).astype(BF16)
    rank = jnp.dot(above, named.astype(BF16), preferred_element_type=F32)
    columns = experts * HALVES * SLOTS
    spread = (iota((experts, columns), 1) // (HALVES * SLOTS) == iota((experts, columns), 0)).astype(BF16)
    order = jnp.dot(((rank + 1.0) * named).astype(BF16), spread, preferred_element_type=F32)
    column = iota((nodes, columns), 1)
    slot = column - (column // SLOTS) * SLOTS
    placed = order == (slot + 1).astype(F32)
    half = (column // SLOTS) - (column // (HALVES * SLOTS)) * HALVES
    return named, spread, placed, half


def combine(rec, state, stats, ids, experts, width):
    nodes = ids.shape[0]
    named, spread, placed, half = routing(ids, experts)
    logits = stats[:, :experts]
    inv_rms = 1.0 / jnp.sqrt(stats[:, experts : experts + 1] / width + EPS)
    chosen = named / (1.0 + jnp.exp(-(logits * inv_rms)))
    weight = chosen / jnp.sum(chosen, axis=1, keepdims=True) * ROUTE_SCALE
    wide = jnp.dot(
        jnp.concatenate(split3(weight), axis=0), spread, preferred_element_type=F32
    )
    zero = jnp.zeros_like(placed, dtype=F32)
    pieces = []
    for h in range(HALVES):
        for piece in range(3):
            part = wide[piece * nodes : (piece + 1) * nodes]
            pieces.append(jnp.where(placed & (half == h), part, zero))
    mixing = jnp.concatenate(pieces, axis=0).astype(BF16)
    mixed = jnp.dot(mixing, rec, preferred_element_type=F32)
    outs = []
    for h in range(HALVES):
        base = h * 3 * nodes
        outs.append(
            mixed[base : base + nodes]
            + mixed[base + nodes : base + 2 * nodes]
            + mixed[base + 2 * nodes : base + 3 * nodes]
        )
    moe_out = jnp.concatenate(outs, axis=1)
    return (state.astype(F32) + moe_out).astype(BF16)


def owner_kernel(depth, depths, experts, width, copies, *refs):
    first, last = depth == 0, depth == depths
    refs = list(refs)
    tables = refs.pop(0)
    top = tables.shape[2] - 1
    if first:
        root = refs.pop(0)[...]
        start = refs.pop(0)[...]
        attn = refs.pop(0)[...].astype(F32)
        for _ in range(3):
            attn = attn + refs.pop(0)[...].astype(F32)
        start = start + attn.astype(BF16).astype(F32).reshape(start.shape)
        base, start = start[1:], start[0]
        router = refs.pop(0)[...].astype(F32)
        product = split3(router * refs.pop(0)[...])
        blank = jnp.zeros((128 - 3 * experts, router.shape[1]), BF16)
        routed = jnp.concatenate([*product, blank], axis=0)
    else:
        rec = refs.pop(0)[...]
        state_ref = refs.pop(0)
        stats = refs.pop(0)[...]
        for _ in range(3):
            stats = stats + refs.pop(0)[...]
    if not first and not last:
        routed = refs.pop(0)[...]
        start = refs.pop(0)[depth - 1]
    if not first:
        drafted_ref = refs.pop(0)
        drafted = combine(rec, state_ref[...], stats, tables[depth - 1][:, :top], experts, width)
        drafted_ref[...] = drafted
    if last:
        return
    out_state, out_stats, outgoing = refs[:3]
    if first:
        refs[3][...] = routed
        refs[4][...] = base
        previous = root.astype(F32)
    else:
        parents = tables[depth][:, top : top + 1]
        wide = drafted.astype(F32)
        previous = jnp.zeros_like(wide)
        for node in range(wide.shape[0]):
            previous = previous + jnp.where(parents == node, wide[node : node + 1, :], 0.0)
    state = (start + previous).astype(BF16)
    out_state[...] = state
    wide = state.astype(F32)
    square = jnp.sum(wide * wide, axis=1, keepdims=True)
    parts = lax.dot_general(
        state, routed, (((1,), (1,)), ((), ())), preferred_element_type=F32
    )
    logits = parts[:, :experts] + parts[:, experts : 2 * experts] + parts[:, 2 * experts : 3 * experts]
    pad = jnp.zeros((wide.shape[0], 128 - experts - 1), F32)
    out_stats[...] = jnp.concatenate([logits, square, pad], axis=1)
    _, _, placed, half = routing(tables[depth][:, :top], experts)
    table = jnp.concatenate(
        [(placed & (half == h)).astype(F32) for h in range(HALVES)], axis=0
    ).astype(BF16)
    part = wide.shape[1] // HALVES
    halves = jnp.concatenate(
        [wide[:, h * part : (h + 1) * part] for h in range(HALVES)], axis=0
    ).astype(BF16)
    sent = lax.dot_general(table, halves, (((0,), (0,)), ((), ())), preferred_element_type=F32)
    sent = sent.reshape(experts, HALVES * SLOTS, part).astype(BF16)
    for copy in range(copies):
        outgoing[:, copy] = sent


def owner_call(depth, depths, experts, width, copies, args, nodes, quarter):
    outs = []
    if depth > 0:
        outs.append(jax.ShapeDtypeStruct((nodes, quarter), BF16))
    if depth < depths:
        outs.append(jax.ShapeDtypeStruct((nodes, quarter), BF16))
        outs.append(jax.ShapeDtypeStruct((nodes, 128), F32))
        outs.append(
            jax.ShapeDtypeStruct((experts, copies, HALVES * SLOTS, quarter // HALVES), BF16)
        )
    if depth == 0:
        outs.append(jax.ShapeDtypeStruct((128, quarter), BF16))
        outs.append(jax.ShapeDtypeStruct((depths - 1, nodes, quarter), F32))
    return pl.pallas_call(
        functools.partial(owner_kernel, depth, depths, experts, width, copies),
        out_shape=outs,
        compiler_params=pltpu.CompilerParams(vmem_limit_bytes=VMEM_BYTES),
    )(*args)


def expert_kernel(width, x_ref, gain_ref, gate_ref, up_ref, act_ref, pack, square, total):
    step = pl.program_id(0)
    sources, quarters, group, part = x_ref.shape
    rows = sources * group
    per_half = rows // HALVES
    hidden = gate_ref.shape[1]

    @pl.when(step == 0)
    def _():
        pack[...] = pack_matrix(rows, True)
        square[...] = jnp.zeros_like(square)
        total[...] = jnp.zeros_like(total)

    each = quarters // 2
    for turn_index in range(each):
        at = step * each + turn_index
        mixed = x_ref[:, at].astype(F32).reshape(rows, part).astype(BF16)
        packed = jnp.dot(pack[...], mixed, preferred_element_type=F32)
        gain = gain_ref[at]
        for h in range(HALVES):
            piece = packed[h * per_half : (h + 1) * per_half]
            square[...] += jnp.sum(piece * piece, axis=1, keepdims=True)
            piece = (piece * gain[h : h + 1, :]).astype(BF16)
            start = (turn_index * HALVES + h) * part
            span = slice(start, start + part)
            total[:, :hidden] += jnp.dot(piece, gate_ref[span, :], preferred_element_type=F32)
            total[:, hidden:] += jnp.dot(piece, up_ref[span, :], preferred_element_type=F32)

    @pl.when(step == pl.num_programs(0) - 1)
    def _():
        inv = 1.0 / jnp.sqrt(square[...] / width + EPS)
        gate = total[:, :hidden] * inv
        act_ref[...] = (gate / (1.0 + jnp.exp(-gate)) * (total[:, hidden:] * inv)).astype(BF16)


def expert_call(width, x, gain, gate, up):
    sources, quarters, group, part = x.shape
    rows = sources * group
    hidden = gate.shape[1]
    block = gate.shape[0] // 2
    return pl.pallas_call(
        functools.partial(expert_kernel, width),
        grid=(2,),
        in_specs=[
            pl.BlockSpec(x.shape, lambda i: (0, 0, 0, 0)),
            pl.BlockSpec(gain.shape, lambda i: (0, 0, 0)),
            pl.BlockSpec((block, hidden), lambda i: (i, 0)),
            pl.BlockSpec((block, hidden), lambda i: (i, 0)),
        ],
        out_specs=pl.BlockSpec((rows // HALVES, hidden), lambda i: (0, 0)),
        out_shape=jax.ShapeDtypeStruct((rows // HALVES, hidden), BF16),
        scratch_shapes=[
            pltpu.VMEM((rows, rows), BF16),
            pltpu.VMEM((rows // HALVES, 1), F32),
            pltpu.VMEM((rows // HALVES, 2 * hidden), F32),
        ],
        compiler_params=pltpu.CompilerParams(vmem_limit_bytes=VMEM_BYTES),
    )(x, gain, gate, up)


def down_kernel(count, *refs):
    acts, weights, out_ref = refs[:count], refs[count : 2 * count], refs[2 * count]
    total = jnp.dot(acts[0][...], weights[0][...], preferred_element_type=F32)
    for index in range(1, count):
        total = total + jnp.dot(acts[index][...], weights[index][...], preferred_element_type=F32)
    part = total.shape[1] // HALVES
    stacked = jnp.concatenate(
        [total[:, h * part : (h + 1) * part] for h in range(HALVES)], axis=0
    ).astype(BF16)
    unpack = pack_matrix(stacked.shape[0], False)
    out_ref[...] = jnp.dot(unpack, stacked, preferred_element_type=F32).astype(BF16)


def down_call(acts, weights):
    rows = acts[0].shape[0]
    quarter = weights[0].shape[1]
    return pl.pallas_call(
        functools.partial(down_kernel, len(acts)),
        out_shape=jax.ShapeDtypeStruct((rows * HALVES, quarter // HALVES), BF16),
        compiler_params=pltpu.CompilerParams(vmem_limit_bytes=VMEM_BYTES),
    )(*acts, *weights)


def turn_kernel(weight_ref, out_ref):
    out_ref[...] = weight_ref[...].T


def turn(weight):
    return pl.pallas_call(
        turn_kernel,
        out_shape=jax.ShapeDtypeStruct(weight.shape[::-1], weight.dtype),
        compiler_params=pltpu.CompilerParams(vmem_limit_bytes=VMEM_BYTES),
    )(weight)


def project_kernel(rows_ref, weight_ref, out_ref):
    columns = jnp.dot(rows_ref[...], weight_ref[...], preferred_element_type=F32)
    out_ref[...] = columns.reshape(out_ref.shape).astype(BF16)


def project(rows, weight, owners):
    steps = 2
    group = rows.shape[0] // owners
    return pl.pallas_call(
        project_kernel,
        grid=(steps,),
        in_specs=[
            pl.BlockSpec((rows.shape[0] // steps, rows.shape[1]), lambda i: (i, 0)),
            pl.BlockSpec(weight.shape, lambda i: (0, 0)),
        ],
        out_specs=pl.BlockSpec((owners // steps, group, weight.shape[1]), lambda i: (i, 0, 0)),
        out_shape=jax.ShapeDtypeStruct((owners, group, weight.shape[1]), BF16),
        compiler_params=pltpu.CompilerParams(vmem_limit_bytes=VMEM_BYTES),
    )(rows, weight)


def settle_kernel(place_ref, x_ref, *refs):
    outs, wide = refs[:-1], refs[-1]
    quarters = len(outs)
    blocks, _, columns = x_ref.shape
    value = x_ref[...].astype(F32)
    per = blocks // quarters
    for block in range(blocks):
        at = (block % per) * columns
        wide[block // per, :, at : at + columns] = value[block]
    for k in range(quarters):
        outs[k][...] = wide[lax.rem(place_ref[0] + k, quarters)].astype(BF16)


def settle(place, x, quarters):
    blocks, rows, columns = x.shape
    width = blocks // quarters * columns
    return pl.pallas_call(
        settle_kernel,
        in_specs=[
            pl.BlockSpec(memory_space=pltpu.SMEM),
            pl.BlockSpec(memory_space=pltpu.VMEM),
        ],
        out_shape=[jax.ShapeDtypeStruct((rows, width), BF16) for _ in range(quarters)],
        scratch_shapes=[pltpu.VMEM((quarters, rows, width), F32)],
        compiler_params=pltpu.CompilerParams(vmem_limit_bytes=VMEM_BYTES),
    )(place, x)


def attend_kernel(scale, length_ref, q_ref, cache_ref, out_ref, highest, summed, total):
    step = pl.program_id(0)
    rows, latent = out_ref.shape
    chunk = cache_ref.shape[1]
    keys = cache_ref[...]
    values = keys[:latent].T
    valid = step * chunk + iota((1, chunk), 1) < length_ref[0]
    block = min(rows, 256)

    @pl.when(step == 0)
    def _():
        highest[...] = jnp.full_like(highest, -1e30)
        summed[...] = jnp.zeros_like(summed)
        total[...] = jnp.zeros_like(total)

    def score(at):
        return jnp.dot(q_ref[at : at + block, :], keys, preferred_element_type=F32)

    ahead = score(0)
    for at in range(0, rows, block):
        span = slice(at, at + block)
        scores = jnp.where(valid, ahead, -1e30)
        if at + block < rows:
            ahead = score(at + block)
        before = highest[span, :]
        now = jnp.maximum(before, jnp.max(scores, axis=1, keepdims=True))
        weights = jnp.exp2((scores - now) * scale)
        fade = jnp.exp2((before - now) * scale)
        highest[span, :] = now
        summed[span, :] = summed[span, :] * fade + jnp.sum(weights, axis=1, keepdims=True)
        total[span, :] = total[span, :] * fade + jnp.dot(
            weights.astype(BF16), values, preferred_element_type=F32
        )

    @pl.when(step == pl.num_programs(0) - 1)
    def _():
        out_ref[...] = (total[...] / summed[...]).astype(BF16)


def attend_request(query_block, cache_block, length, value_up, score_scale):
    depths, nodes, heads_dev, width_qk = query_block.shape
    latent = value_up.shape[1]
    query_rows = query_block.reshape(-1, width_qk)
    rows = query_rows.shape[0]
    chunk = 1024
    latent_out = pl.pallas_call(
        functools.partial(attend_kernel, score_scale * math.log2(math.e)),
        grid=(cache_block.shape[0] // chunk,),
        in_specs=[
            pl.BlockSpec(memory_space=pltpu.SMEM),
            pl.BlockSpec((rows, width_qk), lambda i: (0, 0)),
            pl.BlockSpec((width_qk, chunk), lambda i: (0, i)),
        ],
        out_specs=pl.BlockSpec((rows, latent), lambda i: (0, 0)),
        out_shape=jax.ShapeDtypeStruct((rows, latent), BF16),
        scratch_shapes=[
            pltpu.VMEM((rows, 1), F32),
            pltpu.VMEM((rows, 1), F32),
            pltpu.VMEM((rows, latent), F32),
        ],
        compiler_params=pltpu.CompilerParams(vmem_limit_bytes=VMEM_BYTES),
    )(length, query_rows, cache_block.T)
    latent_out = latent_out.reshape(depths * nodes, heads_dev, latent)
    mixed = jnp.einsum("nhl,hld->nhd", latent_out, value_up, preferred_element_type=F32)
    return mixed.astype(BF16).reshape(depths, nodes, -1)


def local(
    node_embed,
    embed_gain,
    root_hidden,
    parents,
    queries,
    cache,
    cache_len,
    value_up,
    out_proj,
    moe_gain,
    router,
    expert_ids,
    w_gate,
    w_up,
    w_down,
):
    depths, _, nodes, quarter = node_embed.shape
    groups = lax.axis_size("dp")
    tp = lax.axis_size("tp")
    mine = lax.axis_index("tp")
    width = quarter * tp
    part = quarter // HALVES
    experts = router.shape[1]
    latent = value_up.shape[1]
    score_scale = (value_up.shape[2] + cache.shape[2] - latent) ** (-0.5)
    shifts = {k: [(i, (i + k) % tp) for i in range(tp)] for k in range(1, tp)}

    def share(value):
        return [value] + [lax.ppermute(value, "tp", shifts[k]) for k in range(1, tp)]

    def deal(values):
        return [values[0]] + [lax.ppermute(values[k], "tp", shifts[k]) for k in range(1, tp)]

    heads = attend_request(queries[:, 0], cache[0], cache_len, value_up, score_scale)
    heads = heads.reshape(depths * nodes, -1)
    gathered = lax.all_gather(heads, "dp", axis=0, tiled=True)

    w_down, node_embed, heads = lax.optimization_barrier((w_down, node_embed, heads))
    down = deal(
        [
            lax.dynamic_slice(
                w_down[0], (0, (mine + k) % tp * quarter), (w_down.shape[1], quarter)
            )
            for k in range(tp)
        ]
    )
    embed = node_embed[:, 0].astype(F32)
    squares = jnp.sum(embed * embed, axis=-1).reshape(1, depths * nodes)
    gain_rows = quarter // 128
    notes = jnp.concatenate(
        [
            moe_gain.reshape(gain_rows, 128),
            jnp.pad(squares, ((0, 1), (0, 128 - depths * nodes))),
        ]
    )
    notes = jnp.stack(share(notes))
    embed_sq = jnp.sum(notes[:, gain_rows, : depths * nodes], axis=0).reshape(depths, nodes)
    normed = embed * (1.0 / jnp.sqrt(embed_sq / width + EPS))[..., None] * embed_gain
    gains = notes[(mine - jnp.arange(tp, dtype=jnp.int32)) % tp, :gain_rows].reshape(tp, HALVES, part)
    turned, heads = lax.optimization_barrier((out_proj.T, heads))
    turned = turn(turned)
    gathered, normed, gains, turned, *down = lax.optimization_barrier(
        (gathered, normed, gains, turned, *down)
    )
    columns = project(gathered, turned, groups)
    columns = lax.all_to_all(columns, "dp", split_axis=0, concat_axis=0, tiled=True)
    attn = deal(settle(mine.reshape(1).astype(jnp.int32), columns, tp))

    names = jnp.pad(parents[:, 0, :, None], ((1, 0), (0, 0), (0, 0)))
    tables = jnp.concatenate([expert_ids[:, 0], names], axis=2)
    drafted = []
    carried = None
    for depth in range(depths + 1):
        args = [tables]
        if depth == 0:
            args += [root_hidden, normed, *attn, router.T, moe_gain[None]]
        else:
            args += carried
        if 0 < depth < depths:
            args += [routed, base]
        result = list(owner_call(depth, depths, experts, width, tp, args, nodes, quarter))
        if depth > 0:
            drafted.append(result.pop(0))
        if depth == depths:
            break
        if depth == 0:
            routed, base = result.pop(-2), result.pop()
        state, stats, outgoing = result
        all_stats = share(stats)
        outgoing = outgoing.reshape(experts * tp, HALVES * SLOTS, part)
        arrived = lax.all_to_all(outgoing, ("dp", "tp"), split_axis=0, concat_axis=0, tiled=True)
        arrived = arrived.reshape(groups, tp, HALVES * SLOTS, part)
        act = expert_call(width, arrived, gains, w_gate[0], w_up[0])
        answer = down_call(share(act), down)
        answer = answer.reshape(groups, HALVES * SLOTS, part)
        returned = lax.all_to_all(answer, "dp", split_axis=0, concat_axis=0, tiled=True)
        carried = [returned.reshape(groups * HALVES * SLOTS, part), state] + all_stats
    return jnp.stack(drafted)[:, None]


def solution(mesh):
    placed = (
        P(None, "dp", None, "tp"),
        P("tp"),
        P("dp", "tp"),
        P(None, "dp", None),
        P(None, "dp", None, "tp", None),
        P("dp", None, None),
        P("dp"),
        P("tp", None, None),
        P("tp", "dp"),
        P("tp"),
        P("tp", None),
        P(None, "dp", None, None),
        P("dp", None, "tp"),
        P("dp", None, "tp"),
        P("dp", "tp", None),
    )
    return jax.shard_map(
        local, mesh=mesh, in_specs=placed, out_specs=P(None, "dp", None, "tp"), check_vma=False
    )
```
